256 devices in a mesh: dp: 8 (over y_lo, x), fsdp: 32 (over z, y_hi, core).
Axes of the slice: x: 4, y: 4 (y_hi: 2, y_lo: 2; y = y_hi * 2 + y_lo), z: 8, core: 2. Of those that a mesh axis runs over, the one named last changes fastest.
Arguments:
- gradient: bfloat16 [8, 14336, 4096], P('dp', None, 'fsdp'), may hold values from -6 to 6
- error_buffer: bfloat16 [8, 14336, 4096], P('dp', None, 'fsdp'), may hold values from -4 to 4
- q_start: float32 [4096, 64], P('fsdp'), may hold values from -6 to 6
Outputs:
- new_error: bfloat16 [8, 14336, 4096], P('dp', None, 'fsdp')
- q_factor: float32 [4096, 64], P('fsdp')
The draws below stay inside these ranges and needn't reach their ends.
All inputs are finite; a program needn't handle non-finite values.
Results may differ from the reference program's by a relative error of at most 0.0013.
Values sent between devices are 32-bit elements; how exact they have to be, the bound alone decides.
A program may use at most 64 MiB of HBM per device.

```python
import jax
import jax.numpy as jnp
from jax import lax

FF = 14336
RANK = 64
ITERS = 2
D = 4096
N_DP = 8


def with_spikes(values, own_key, source, target, blocks, factor):
    owner, partner = [(jnp.arange(values.shape[position]) // (values.shape[position] // blocks)).reshape([-1 if axis == position else 1 for axis in range(values.ndim)]) for position in (source, target)]
    chosen = jax.random.permutation(own_key, blocks)[partner]
    strong = (owner == chosen) | (owner == (partner + blocks // 2) % blocks)
    return jnp.where(strong, factor * values, values)


def shard_levels(rng, shape, cuts, least, top_value):
    loudness, own = 1.0, jax.random.fold_in(rng, 6)
    for axis_at, blocks in cuts:
        heights = jnp.exp(jax.random.uniform(jax.random.fold_in(own, axis_at), (blocks,), jnp.float32, least / len(cuts), top_value / len(cuts)))
        loudness = loudness * jnp.repeat(heights, shape[axis_at] // blocks).reshape([-1 if axis == axis_at else 1 for axis in range(len(shape))])
    return loudness


def noise(key, shape, scale, reach, shards=(), kind=jnp.bfloat16):
    factor_of = shard_levels(key, shape, shards, -0.22, 0.18) if shards else 1.0
    drawn = jax.random.normal(key, shape, jnp.float32) * scale * factor_of
    return jnp.minimum(jnp.maximum(drawn, -reach), reach).astype(kind)


def heavy_noise(key, shape, spread, reach, shards, heavy, kind=jnp.bfloat16):
    result = spread * jax.random.normal(key, shape, jnp.float32)
    if shards:
        result = result * shard_levels(key, shape, shards, -0.22, 0.18)
    return jnp.clip(with_spikes(result, jax.random.fold_in(key, 3), *heavy), -reach, reach).astype(kind)


def setup_inputs(seed: int = 0) -> dict:
    key_of = jax.random.split(jax.random.key(seed), 4)
    gradient = heavy_noise(key_of[0], (N_DP, FF, D), 1.0, 6.0, ((0, 8), (2, 32)), (2, 1, 32, 2.75))
    error_buffer = noise(key_of[1], (N_DP, FF, D), 0.5, 4.0, ((0, 8), (2, 32)))
    q_start = noise(key_of[2], (D, RANK), 1.0, 6.0, ((0, 32),), jnp.float32)
    return dict(gradient=gradient, error_buffer=error_buffer, q_start=q_start)


def orthonormal(left, gram):
    lower = jnp.linalg.cholesky(gram)
    inverse = jax.scipy.linalg.solve_triangular(lower, jnp.eye(gram.shape[0], dtype=jnp.float32), lower=True)
    return jnp.dot(left, inverse.T, precision=lax.Precision.HIGHEST)

def reference(gradient, error_buffer, q_start):
    highest = lax.Precision.HIGHEST
    replicas = gradient.shape[0]
    q_now = q_start
    basis = None
    for step in range(ITERS):
        left = jnp.zeros((FF, RANK), jnp.float32)
        for member in range(replicas):
            accum = gradient[member].astype(jnp.float32) + error_buffer[member].astype(jnp.float32)
            left = left + jnp.dot(accum, q_now, precision=highest)
        left = left / replicas
        gram = jnp.dot(left.T, left, precision=highest)
        basis = orthonormal(left, gram)
        right = jnp.zeros((D, RANK), jnp.float32)
        for member in range(replicas):
            accum = gradient[member].astype(jnp.float32) + error_buffer[member].astype(jnp.float32)
            right = right + jnp.dot(accum.T, basis, precision=highest)
        q_now = right / replicas
    update = jnp.dot(basis, q_now.T, precision=highest)
    errors = []
    for member in range(replicas):
        accum = gradient[member].astype(jnp.float32) + error_buffer[member].astype(jnp.float32)
        errors.append((accum - update).astype(jnp.bfloat16))
    return (jnp.stack(errors, 0), q_now)
```

```python
import functools

import jax
import jax.numpy as jnp
from jax import lax
from jax.experimental import pallas as pl
from jax.experimental.pallas import tpu as pltpu
from jax.sharding import PartitionSpec as P

ITERS = 2
RANK = 64
LANES = 128
SUB = 8
PER = 7
USED = 2 * PER
SLOTS = 16
YL = 2
MESH = pl.DeviceIdType.MESH


def split3(value):
    hi = value.astype(jnp.bfloat16)
    rest = value - hi.astype(jnp.float32)
    mid = rest.astype(jnp.bfloat16)
    lo = (rest - mid.astype(jnp.float32)).astype(jnp.bfloat16)
    return hi, mid, lo


def dot(a, b, dims, precision=None):
    return lax.dot_general(
        a, b, (dims, ((), ())), precision=precision, preferred_element_type=jnp.float32
    )


def inverse_factor(gram):
    rank = gram.shape[0]
    rows = lax.broadcasted_iota(jnp.int32, (rank, rank), 0)
    cols = lax.broadcasted_iota(jnp.int32, (rank, rank), 1)
    eye = (rows == cols).astype(jnp.float32)
    work = jnp.concatenate([gram, eye], axis=1)
    below = lax.broadcasted_iota(jnp.int32, (rank, 1), 0)
    done = []
    for k in range(rank):
        first = (k // SUB) * SUB
        row = work[k - first : k - first + 1, :]
        factor = work[:, k : k + 1] / row[:, k : k + 1]
        factor = jnp.where(below[first:] > k, factor, 0.0)
        work = work - factor * row
        if k % SUB == SUB - 1:
            done.append(work[:SUB])
            work = work[SUB:]
    work = jnp.concatenate(done, axis=0)
    pivots = jnp.sum(work[:, :rank] * eye, axis=1, keepdims=True)
    return work[:, rank:] / jnp.sqrt(pivots)


def iteration(sizes, g_ref, e_ref, q_ref, o_ref, qn_ref, w_ref,
              p, r0, r1a, r1b, r2a, r2b, r3, rq, acc, gacc, send, recv):
    nx, ny, nz = sizes
    chunks = nx * ny
    zhalf = nz // 2
    zt = SLOTS // zhalf
    dp = lax.axis_index("dp")
    fs = lax.axis_index("fsdp")
    x = lax.rem(dp, nx)
    ylo = dp // nx
    yh = ny // YL
    core = lax.rem(fs, 2)
    yhi = lax.rem(fs // 2, yh)
    z = fs // (2 * yh)
    y = yhi * YL + ylo

    def device(dx, dy, dz, dc):
        tx = lax.rem(x + dx, nx)
        ty = lax.rem(y + dy, ny)
        tz = lax.rem(z + dz, nz)
        tc = lax.rem(core + dc, 2)
        return (lax.rem(ty, YL) * nx + tx, (tz * yh + ty // YL) * 2 + tc)

    def replica(d):
        return (lax.rem(dp + d, YL * nx), fs)

    peers = [device(0, 0, 0, 1)]
    peers += [device(d, 0, 0, 0) for d in range(1, nx)]
    peers += [device(0, d, 0, 0) for d in range(1, ny)]
    peers += [device(0, 0, d, 0) for d in range(1, nz)]
    peers += [
        (lax.rem(ylo + 1, YL) * nx + lax.rem(x + d, nx), fs) for d in range(1, nx)
    ]
    barrier = pltpu.get_barrier_semaphore()
    for peer in peers:
        pl.semaphore_signal(barrier, inc=1, device_id=peer, device_id_type=MESH)
    pl.semaphore_wait(barrier, len(peers))

    count = [0]

    def push(src, dst, target):
        n = count[0]
        count[0] += 1
        copy = pltpu.make_async_remote_copy(
            src_ref=src, dst_ref=dst, send_sem=send.at[n], recv_sem=recv.at[n],
            device_id=target, device_id_type=MESH,
        )
        copy.start()
        return copy

    def finish(copies):
        for copy in copies:
            copy.wait()

    parts = split3(q_ref[...].T)
    left = jnp.concatenate([jnp.concatenate([v, v], axis=1) for v in parts], axis=0)
    step_tiles = 2 * PER
    step_rows = step_tiles * LANES

    def tile_at(k, j):
        return 2 * k + j // PER, pl.ds((j % PER) * 2, 2)

    def both(k):
        rows = pl.ds(pl.multiple_of(k * step_rows, step_rows), step_rows)
        return jnp.concatenate([g_ref[rows, :], e_ref[rows, :]], axis=1)

    def project(k, carry):
        out = dot(left, both(k), ((1,), (1,)))
        out = out[:RANK] + out[RANK : 2 * RANK] + out[2 * RANK :]
        for j in range(step_tiles):
            chunk, slots = tile_at(k, j)
            tile = out[:, j * LANES : (j + 1) * LANES]
            p[:, :, chunk, slots] = tile.reshape(2, 2, 2, SUB, LANES)
        for half in range(2):
            p[:, :, 2 * k + half, USED:] = jnp.zeros(
                (2, 2, SLOTS - USED, SUB, LANES), jnp.float32
            )
        return carry

    lax.fori_loop(0, chunks // 2, project, 0)

    used = pl.ds(0, USED)
    other = lax.rem(core + 1, 2)
    finish([push(p.at[other, :, :, used], r0, device(0, 0, 0, 1))])

    def add_core(k, carry):
        p[core, :, k, :USED] += r0[:, k]
        return carry

    lax.fori_loop(0, chunks, add_core, 0)

    def at_x(d):
        return lax.rem(x + d, nx)

    def at_y(d):
        return lax.rem(y + d, ny)

    copies = []
    for d in range(1, nx):
        src = p.at[core, 0, pl.ds(at_x(d) * ny, ny), used]
        copies.append(push(src, r1a.at[d - 1], device(d, 0, 0, 0)))
    for d in range(1, ny):
        src = p.at[core, 1, pl.ds(at_y(d) * nx, nx), used]
        copies.append(push(src, r1b.at[d - 1], device(0, d, 0, 0)))
    finish(copies)

    def add_a(k, carry):
        total = p[core, 0, x * ny + k, :USED]
        for d in range(nx - 1):
            total = total + r1a[d, k]
        p[core, 0, x * ny + k, :USED] = total
        return carry

    def add_b(k, carry):
        total = p[core, 1, y * nx + k, :USED]
        for d in range(ny - 1):
            total = total + r1b[d, k]
        p[core, 1, y * nx + k, :USED] = total
        return carry

    lax.fori_loop(0, ny, add_a, 0)
    lax.fori_loop(0, nx, add_b, 0)

    copies = []
    for d in range(1, ny):
        src = p.at[core, 0, x * ny + at_y(d), used]
        copies.append(push(src, r2a.at[d - 1], device(0, d, 0, 0)))
    for d in range(1, nx):
        src = p.at[core, 1, y * nx + at_x(d), used]
        copies.append(push(src, r2b.at[d - 1], device(d, 0, 0, 0)))
    finish(copies)
    mine_a = x * ny + y
    mine_b = y * nx + x
    total = p[core, 0, mine_a, :USED]
    for d in range(ny - 1):
        total = total + r2a[d]
    p[core, 0, mine_a, :USED] = total
    total = p[core, 1, mine_b, :USED]
    for d in range(nx - 1):
        total = total + r2b[d]
    p[core, 1, mine_b, :USED] = total

    def z_block(ref, zz):
        part = zz // zhalf
        chunk = part * mine_b + (1 - part) * mine_a
        return ref.at[core, part, chunk, pl.ds(lax.rem(zz, zhalf) * zt, zt)]

    copies = []
    for d in range(1, nz):
        src = z_block(p, lax.rem(z + d, nz))
        copies.append(push(src, r3.at[d - 1], device(0, 0, d, 0)))
    finish(copies)
    total = z_block(p, z)[...]
    for d in range(nz - 1):
        total = total + r3[d]
    z_block(o_ref, z)[...] = total

    mine = z_block(o_ref, z)
    finish([push(mine, mine, device(0, 0, d, 0)) for d in range(1, nz)])
    mine = o_ref.at[core, 0, mine_a, used]
    copies = [push(mine, mine, device(0, d, 0, 0)) for d in range(1, ny)]
    mine = o_ref.at[core, 1, mine_b, used]
    copies += [push(mine, mine, device(d, 0, 0, 0)) for d in range(1, nx)]
    finish(copies)
    mine = o_ref.at[core, 0, pl.ds(x * ny, ny), used]
    copies = [push(mine, mine, device(d, 0, 0, 0)) for d in range(1, nx)]
    mine = o_ref.at[core, 1, pl.ds(y * nx, nx), used]
    copies += [push(mine, mine, device(0, d, 0, 0)) for d in range(1, ny)]
    finish(copies)
    mine = o_ref.at[core, :, :, used]
    finish([push(mine, mine, device(0, 0, 0, 1))])

    acc[...] = jnp.zeros_like(acc)
    gacc[...] = jnp.zeros_like(gacc)

    def back(k, carry):
        tiles = []
        for j in range(step_tiles):
            chunk, slots = tile_at(k, j)
            tiles.append(o_ref[:, :, chunk, slots].reshape(RANK, LANES))
        stack = jnp.concatenate(split3(jnp.concatenate(tiles, axis=1)), axis=0)
        acc[...] += dot(stack, both(k), ((1,), (0,)))
        gacc[...] += dot(stack, stack, ((1,), (1,)))
        return carry

    lax.fori_loop(0, chunks // 2, back, 0)
    right = acc[...]
    right = right[:, :LANES] + right[:, LANES:]
    right = right[:RANK] + right[RANK : 2 * RANK] + right[2 * RANK :]
    replicas = YL * nx
    rq[dp] = right
    copies = [push(rq.at[dp], rq.at[dp], replica(d)) for d in range(1, replicas)]

    gram = gacc[...]
    gram = gram[:, :RANK] + gram[:, RANK : 2 * RANK] + gram[:, 2 * RANK :]
    gram = gram[:RANK] + gram[RANK : 2 * RANK] + gram[2 * RANK :]
    inverse = inverse_factor(gram / (replicas * replicas))
    finish(copies)
    right = rq[0]
    for d in range(1, replicas):
        right = right + rq[d]
    right = right / (replicas * replicas)
    q_next = dot(inverse, right, ((1,), (0,)), lax.Precision.HIGHEST)
    qn_ref[...] = q_next.T
    w_ref[...] = dot(inverse, q_next, ((0,), (0,)), lax.Precision.HIGHEST) / replicas


def run_iteration(sizes, gradient, error_buffer, q_now):
    nx, ny, nz = sizes
    chunks = nx * ny
    f32 = jnp.float32
    replicas = YL * nx
    copies = 2 + 4 * (nx - 1) + 4 * (ny - 1) + 2 * (nz - 1) + replicas - 1
    vmem = pl.BlockSpec(memory_space=pltpu.VMEM)
    tile = (SUB, LANES)
    rows = gradient.shape[0]
    return pl.pallas_call(
        functools.partial(iteration, sizes),
        out_shape=(
            jax.ShapeDtypeStruct((2, 2, chunks, SLOTS) + tile, f32),
            jax.ShapeDtypeStruct(q_now.shape, f32),
            jax.ShapeDtypeStruct((RANK, LANES), f32),
        ),
        in_specs=[vmem] * 3,
        out_specs=(vmem,) * 3,
        scratch_shapes=[
            pltpu.VMEM((2, 2, chunks, SLOTS) + tile, f32),
            pltpu.VMEM((2, chunks, USED) + tile, f32),
            pltpu.VMEM((nx - 1, ny, USED) + tile, f32),
            pltpu.VMEM((ny - 1, nx, USED) + tile, f32),
            pltpu.VMEM((ny - 1, USED) + tile, f32),
            pltpu.VMEM((nx - 1, USED) + tile, f32),
            pltpu.VMEM((nz - 1, SLOTS // (nz // 2)) + tile, f32),
            pltpu.VMEM((replicas, RANK, LANES), f32),
            pltpu.VMEM((3 * RANK, 2 * LANES), f32),
            pltpu.VMEM((3 * RANK, 3 * RANK), f32),
            pltpu.SemaphoreType.DMA((copies,)),
            pltpu.SemaphoreType.DMA((copies,)),
        ],
        compiler_params=pltpu.CompilerParams(
            collective_id=0, has_side_effects=True, vmem_limit_bytes=48 * 2**20
        ),
        cost_estimate=pl.CostEstimate(
            flops=8 * rows * LANES * RANK, bytes_accessed=12 * rows * LANES,
            transcendentals=0,
        ),
    )(gradient, error_buffer, q_now)


def finish_kernel(o_ref, w_ref, g_ref, e_ref, out_ref):
    hi, mid, _ = split3(w_ref[...])
    right = jnp.concatenate([hi, hi, mid], axis=0)
    for j in range(PER):
        tile = o_ref[:, :, 0, 2 * j : 2 * j + 2].reshape(RANK, LANES)
        hi, mid, _ = split3(tile)
        left = jnp.concatenate([hi, mid, hi], axis=0)
        update = dot(left, right, ((0,), (0,)))
        rows = pl.ds(j * LANES, LANES)
        accum = g_ref[rows, :].astype(jnp.float32) + e_ref[rows, :].astype(jnp.float32)
        out_ref[rows, :] = (accum - update).astype(jnp.bfloat16)


def run_finish(left, weight, gradient, error_buffer):
    chunks = left.shape[2]
    rows = gradient.shape[0]
    block = pl.BlockSpec((PER * LANES, LANES), lambda i: (i, 0))
    return pl.pallas_call(
        finish_kernel,
        grid=(chunks,),
        out_shape=jax.ShapeDtypeStruct(gradient.shape, jnp.bfloat16),
        in_specs=[
            pl.BlockSpec((2, 2, 1, SLOTS, SUB, LANES), lambda i: (0, 0, i, 0, 0, 0)),
            pl.BlockSpec((RANK, LANES), lambda i: (0, 0)),
            block,
            block,
        ],
        out_specs=block,
        cost_estimate=pl.CostEstimate(
            flops=2 * rows * LANES * RANK, bytes_accessed=10 * rows * LANES,
            transcendentals=0,
        ),
    )(left, weight, gradient, error_buffer)


def on_device(sizes, gradient, error_buffer, q_start):
    gradient, error_buffer, q_now = gradient[0], error_buffer[0], q_start
    for _ in range(ITERS):
        left, q_now, weight = run_iteration(sizes, gradient, error_buffer, q_now)
    new_error = run_finish(left, weight, gradient, error_buffer)
    return (new_error[None], q_now)


def solution(mesh, sizes=(4, 4, 8)):
    in_specs = (P("dp", None, "fsdp"), P("dp", None, "fsdp"), P("fsdp", None))
    out_specs = (P("dp", None, "fsdp"), P("fsdp", None))
    return jax.shard_map(
        functools.partial(on_device, sizes), mesh=mesh, in_specs=in_specs,
        out_specs=out_specs, check_vma=False,
    )
```

```python
import functools

import jax
import jax.numpy as jnp
from jax import lax
from jax.experimental import pallas as pl
from jax.experimental.pallas import tpu as pltpu
from jax.sharding import PartitionSpec as P

ITERS = 2
RANK = 64
LANES = 128
SUB = 8
PER = 7
SLOTS = 8
BATCHES = 2
YL = 2
MESH = pl.DeviceIdType.MESH
HIGHEST = lax.Precision.HIGHEST
F32 = jnp.float32
BF16 = jnp.bfloat16


def split3(value):
    hi = value.astype(BF16)
    rest = value - hi.astype(F32)
    mid = rest.astype(BF16)
    lo = (rest - mid.astype(F32)).astype(BF16)
    return hi, mid, lo


def dot(a, b, dims, precision=None):
    return lax.dot_general(
        a, b, (dims, ((), ())), precision=precision, preferred_element_type=F32
    )


def inverse_factor(gram):
    rank = gram.shape[0]
    rows = lax.broadcasted_iota(jnp.int32, (rank, rank), 0)
    cols = lax.broadcasted_iota(jnp.int32, (rank, rank), 1)
    eye = (rows == cols).astype(F32)
    work = jnp.concatenate([gram, eye], axis=1)
    below = lax.broadcasted_iota(jnp.int32, (rank, 1), 0)
    done = []
    for k in range(rank):
        first = (k // SUB) * SUB
        row = work[k - first : k - first + 1, :]
        factor = work[:, k : k + 1] / row[:, k : k + 1]
        factor = jnp.where(below[first:] > k, factor, 0.0)
        work = work - factor * row
        if k % SUB == SUB - 1:
            done.append(work[:SUB])
            work = work[SUB:]
    work = jnp.concatenate(done, axis=0)
    pivots = jnp.sum(work[:, :rank] * eye, axis=1, keepdims=True)
    return work[:, rank:] / jnp.sqrt(pivots)


def kernel(sizes, g_hbm, e_hbm, q_ref, out_hbm, qn_ref,
           g_ref, e_ref, p, o, r0, r1a, r1b, r2a, r2b, r3, rq, acc, gacc, qt, inv,
           turned, result, load, store, send, recv):
    nx, ny, nz = sizes
    jcs = nx * ny // 2
    zhalf = nz // 2
    zt = SLOTS // zhalf
    dp = lax.axis_index("dp")
    fs = lax.axis_index("fsdp")
    x = lax.rem(dp, nx)
    ylo = dp // nx
    yh = ny // YL
    core = lax.rem(fs, 2)
    yhi = lax.rem(fs // 2, yh)
    z = fs // (2 * yh)
    y = yhi * YL + ylo
    other = lax.rem(core + 1, 2)
    replicas = YL * nx
    batch_rows = jcs * PER * LANES

    loads = []
    for b in range(BATCHES):
        rows = pl.ds(b * batch_rows, batch_rows)
        for n, (src, dst) in enumerate(((g_hbm, g_ref), (e_hbm, e_ref))):
            copy = pltpu.make_async_copy(src.at[rows], dst.at[rows], load.at[2 * b + n])
            copy.start()
            loads.append(copy)

    def device(dx, dy, dz, dc):
        tx = lax.rem(x + dx, nx)
        ty = lax.rem(y + dy, ny)
        tz = lax.rem(z + dz, nz)
        tc = lax.rem(core + dc, 2)
        return (lax.rem(ty, YL) * nx + tx, (tz * yh + ty // YL) * 2 + tc)

    def replica(d):
        return (lax.rem(dp + d, replicas), fs)

    peers = [device(0, 0, 0, 1)]
    peers += [device(d, 0, 0, 0) for d in range(1, nx)]
    peers += [device(0, d, 0, 0) for d in range(1, ny)]
    peers += [device(0, 0, d, 0) for d in range(1, nz)]
    peers += [
        (lax.rem(ylo + 1, YL) * nx + lax.rem(x + d, nx), fs) for d in range(1, nx)
    ]
    barrier = pltpu.get_barrier_semaphore()
    for peer in peers:
        pl.semaphore_signal(barrier, inc=1, device_id=peer, device_id_type=MESH)

    qt[...] = q_ref[...]
    pad = jnp.zeros((2, 2, 2, jcs, SLOTS - PER, SUB, LANES), F32)
    for b in range(BATCHES):
        p[b, :, :, :, :, PER:] = pad
    pl.semaphore_wait(barrier, len(peers))

    used = pl.ds(0, PER)

    def at(index):
        return index // jcs, lax.rem(index, jcs)

    mine = (at(x * ny + y), at(y * nx + x))

    def both(b, start, size):
        rows = pl.ds(pl.multiple_of(b * batch_rows + start, LANES), size)
        return jnp.concatenate([g_ref[rows, :], e_ref[rows, :]], axis=1)

    def z_block(ref, b, zz):
        part = zz // zhalf
        hi = part * mine[1][0] + (1 - part) * mine[0][0]
        jc = part * mine[1][1] + (1 - part) * mine[0][1]
        return ref.at[b, core, part, hi, jc, pl.ds(lax.rem(zz, zhalf) * zt, zt)]

    def row_of(ref, b, part, chip):
        hi, jc = at(chip * (ny, nx)[part])
        return ref.at[b, core, part, hi, pl.ds(jc, (ny, nx)[part]), used]

    def one_of(ref, b, part, index):
        hi, jc = at(index)
        return ref.at[b, core, part, hi, jc, used]

    def one_iteration(it, carry):
        count = [0]

        def push(src, dst, target):
            n = count[0]
            count[0] += 1
            copy = pltpu.make_async_remote_copy(
                src_ref=src, dst_ref=dst, send_sem=send.at[n], recv_sem=recv.at[n],
                device_id=target, device_id_type=MESH,
            )
            copy.start()
            return copy

        def finish(copies):
            for copy in copies:
                copy.wait()

        parts = split3(qt[...])
        left = jnp.concatenate(
            [jnp.concatenate([v, v], axis=1) for v in parts], axis=0
        )
        wide = 2 * PER * LANES

        def project(b, first, last):
            def step(k, c):
                out = dot(left, both(b, k * wide, wide), ((1,), (1,)))
                out = out[:RANK] + out[RANK : 2 * RANK] + out[2 * RANK :]
                for j in range(2 * PER):
                    tile = out[:, j * LANES : (j + 1) * LANES]
                    p[b, :, :, :, 2 * k + j // PER, j % PER] = tile.reshape(
                        2, 2, 2, SUB, LANES
                    )
                return c

            lax.fori_loop(first, last, step, 0)

        half = jcs // 2

        def core_send(b, h):
            src = p.at[b, other, :, :, pl.ds(h * half, half), used]
            return push(src, r0.at[b, h], device(0, 0, 0, 1))

        def core_add(b, h):
            def step(k, c):
                jc = h * half + k
                p[b, core, :, :, jc, :PER] += r0[b, h, :, :, k]
                return c

            lax.fori_loop(0, half, step, 0)

        def first_send(b):
            copies = []
            for d in range(1, max(nx, ny)):
                if d < nx:
                    src = row_of(p, b, 0, lax.rem(x + d, nx))
                    copies.append(push(src, r1a.at[b, d - 1], device(d, 0, 0, 0)))
                if d < ny:
                    src = row_of(p, b, 1, lax.rem(y + d, ny))
                    copies.append(push(src, r1b.at[b, d - 1], device(0, d, 0, 0)))
            return copies

        def first_add(b):
            for part, chip, got, peers in ((0, x, r1a, nx - 1), (1, y, r1b, ny - 1)):
                target = row_of(p, b, part, chip)
                total = target[...]
                for d in range(peers):
                    total = total + got[b, d]
                target[...] = total

        def second_send(b):
            copies = []
            for d in range(1, max(nx, ny)):
                if d < ny:
                    src = one_of(p, b, 0, x * ny + lax.rem(y + d, ny))
                    copies.append(push(src, r2a.at[b, d - 1], device(0, d, 0, 0)))
                if d < nx:
                    src = one_of(p, b, 1, y * nx + lax.rem(x + d, nx))
                    copies.append(push(src, r2b.at[b, d - 1], device(d, 0, 0, 0)))
            return copies

        def second_add(b):
            for part, got, peers in ((0, r2a, ny - 1), (1, r2b, nx - 1)):
                target = p.at[b, core, part, mine[part][0], mine[part][1], used]
                total = target[...]
                for d in range(peers):
                    total = total + got[b, d]
                target[...] = total

        def z_send(b):
            copies = []
            for d in range(1, nz):
                src = z_block(p, b, lax.rem(z + d, nz))
                copies.append(push(src, r3.at[b, d - 1], device(0, 0, d, 0)))
            return copies

        def z_add(b):
            total = z_block(p, b, z)[...]
            for d in range(nz - 1):
                total = total + r3[b, d]
            z_block(o, b, z)[...] = total

        def z_spread(b):
            block = z_block(o, b, z)
            return [push(block, block, device(0, 0, d, 0)) for d in range(1, nz)]

        def second_spread(b):
            copies = []
            one = [one_of(o, b, 0, x * ny + y), one_of(o, b, 1, y * nx + x)]
            for d in range(1, max(nx, ny)):
                if d < ny:
                    copies.append(push(one[0], one[0], device(0, d, 0, 0)))
                if d < nx:
                    copies.append(push(one[1], one[1], device(d, 0, 0, 0)))
            return copies

        def first_spread(b):
            copies = []
            row = [row_of(o, b, 0, x), row_of(o, b, 1, y)]
            for d in range(1, max(nx, ny)):
                if d < nx:
                    copies.append(push(row[0], row[0], device(d, 0, 0, 0)))
                if d < ny:
                    copies.append(push(row[1], row[1], device(0, d, 0, 0)))
            return copies

        def core_spread(b):
            block = o.at[b, core, :, :, :, used]
            return [push(block, block, device(0, 0, 0, 1))]

        def tiles_of(b, jc):
            return [o[b, :, :, :, jc, s].reshape(RANK, LANES) for s in range(PER)]

        def back(b):
            span = half * PER * LANES

            def step(k, c):
                tiles = []
                for i in range(half):
                    tiles += tiles_of(b, k * half + i)
                stack = jnp.concatenate(split3(jnp.concatenate(tiles, axis=1)), axis=0)
                acc[...] += dot(stack, both(b, k * span, span), ((1,), (0,)))
                gacc[...] += dot(stack, stack, ((1,), (1,)))
                return c

            lax.fori_loop(0, 2, step, 0)

        def turn(b):
            @pl.when(it == ITERS - 1)
            def _():
                def step(jc, c):
                    for s, tile in enumerate(tiles_of(b, jc)):
                        hi = tile.astype(BF16).astype(F32)
                        pair = jnp.concatenate([hi, tile - hi], axis=0)
                        start = b * batch_rows + (jc * PER + s) * LANES
                        rows = pl.ds(pl.multiple_of(start, LANES), LANES)
                        turned[rows, :] = pair.T.astype(BF16)
                    return c

                lax.fori_loop(0, jcs, step, 0)

        def loaded(b):
            @pl.when(it == 0)
            def _():
                loads[2 * b].wait()
                loads[2 * b + 1].wait()

        acc[...] = jnp.zeros_like(acc)
        gacc[...] = jnp.zeros_like(gacc)
        steps = jcs // 2
        loaded(0)
        project(0, 0, steps // 2)
        c00 = core_send(0, 0)
        project(0, steps // 2, steps)
        c01 = core_send(0, 1)
        loaded(1)
        project(1, 0, steps // 2)
        c10 = core_send(1, 0)
        c00.wait()
        core_add(0, 0)
        c01.wait()
        core_add(0, 1)
        first0 = first_send(0)
        project(1, steps // 2, steps)
        c11 = core_send(1, 1)
        c10.wait()
        core_add(1, 0)
        c11.wait()
        core_add(1, 1)
        finish(first0)
        first_add(0)
        second0 = second_send(0)
        first1 = first_send(1)
        finish(second0)
        second_add(0)
        z0 = z_send(0)
        finish(first1)
        first_add(1)
        second1 = second_send(1)
        finish(z0)
        z_add(0)
        spread0 = z_spread(0)
        finish(second1)
        second_add(1)
        z1 = z_send(1)
        finish(spread0)
        back0 = second_spread(0)
        finish(z1)
        z_add(1)
        spread1 = z_spread(1)
        finish(back0)
        wide0 = first_spread(0)
        finish(spread1)
        back1 = second_spread(1)
        finish(wide0)
        core0 = core_spread(0)
        finish(back1)
        wide1 = first_spread(1)
        finish(core0)
        back(0)
        turn(0)
        finish(wide1)
        core1 = core_spread(1)
        finish(core1)
        back(1)

        right = acc[...]
        right = right[:, :LANES] + right[:, LANES:]
        right = right[:RANK] + right[RANK : 2 * RANK] + right[2 * RANK :]
        rq[dp] = right
        copies = [push(rq.at[dp], rq.at[dp], replica(d)) for d in range(1, replicas)]
        gram = gacc[...]
        gram = gram[:, :RANK] + gram[:, RANK : 2 * RANK] + gram[:, 2 * RANK :]
        gram = gram[:RANK] + gram[RANK : 2 * RANK] + gram[2 * RANK :]
        inverse = inverse_factor(gram / (replicas * replicas))
        inv[...] = inverse
        turn(1)
        finish(copies)
        right = rq[0]
        for d in range(1, replicas):
            right = right + rq[d]
        right = right / (replicas * replicas)
        qt[...] = dot(inverse, right, ((1,), (0,)), HIGHEST)
        return carry

    lax.fori_loop(0, ITERS, one_iteration, 0)

    q_now = qt[...]
    qn_ref[...] = q_now
    weight = dot(inv[...], q_now, ((0,), (0,)), HIGHEST) / replicas
    hi, mid, _ = split3(weight)
    right = jnp.concatenate(
        [jnp.concatenate([hi, mid], 1), jnp.concatenate([hi, jnp.zeros_like(hi)], 1)], 0
    )
    span = 2 * PER * LANES
    steps = BATCHES * batch_rows // span

    def stored(k):
        rows = pl.ds(pl.multiple_of(k * span, span), span)
        return pltpu.make_async_copy(result.at[rows], out_hbm.at[rows], store.at[k])

    def subtract(k, c):
        rows = pl.ds(pl.multiple_of(k * span, span), span)
        update = dot(turned[rows, :], right, ((1,), (0,)))
        update = update[:, :LANES] + update[:, LANES:]
        accum = g_ref[rows, :].astype(F32) + e_ref[rows, :].astype(F32)
        result[rows, :] = (accum - update).astype(BF16)
        stored(k).start()
        return c

    lax.fori_loop(0, steps, subtract, 0)
    for k in range(steps):
        stored(k).wait()


def on_device(sizes, gradient, error_buffer, q_start):
    nx, ny, nz = sizes
    jcs = nx * ny // 2
    replicas = YL * nx
    per_batch = 3 + 4 * (nx - 1) + 4 * (ny - 1) + 2 * (nz - 1)
    copies = BATCHES * per_batch + replicas - 1
    vmem = pl.BlockSpec(memory_space=pltpu.VMEM)
    hbm = pl.BlockSpec(memory_space=pl.ANY)
    tile = (SUB, LANES)
    gradient, error_buffer = gradient[0], error_buffer[0]
    rows = gradient.shape[0]
    held = pltpu.VMEM((BATCHES, 2, 2, 2, jcs, SLOTS) + tile, F32)
    whole = pltpu.VMEM((rows, LANES), BF16)
    new_error, q_factor = pl.pallas_call(
        functools.partial(kernel, sizes),
        out_shape=(
            jax.ShapeDtypeStruct(gradient.shape, BF16),
            jax.ShapeDtypeStruct((RANK, LANES), F32),
        ),
        in_specs=[hbm, hbm, vmem],
        out_specs=(hbm, vmem),
        scratch_shapes=[
            whole,
            whole,
            held,
            held,
            pltpu.VMEM((BATCHES, 2, 2, 2, jcs // 2, PER) + tile, F32),
            pltpu.VMEM((BATCHES, nx - 1, ny, PER) + tile, F32),
            pltpu.VMEM((BATCHES, ny - 1, nx, PER) + tile, F32),
            pltpu.VMEM((BATCHES, ny - 1, PER) + tile, F32),
            pltpu.VMEM((BATCHES, nx - 1, PER) + tile, F32),
            pltpu.VMEM((BATCHES, nz - 1, SLOTS // (nz // 2)) + tile, F32),
            pltpu.VMEM((replicas, RANK, LANES), F32),
            pltpu.VMEM((3 * RANK, 2 * LANES), F32),
            pltpu.VMEM((3 * RANK, 3 * RANK), F32),
            pltpu.VMEM((RANK, LANES), F32),
            pltpu.VMEM((RANK, RANK), F32),
            whole,
            whole,
            pltpu.SemaphoreType.DMA((2 * BATCHES,)),
            pltpu.SemaphoreType.DMA((jcs,)),
            pltpu.SemaphoreType.DMA((copies,)),
            pltpu.SemaphoreType.DMA((copies,)),
        ],
        compiler_params=pltpu.CompilerParams(
            collective_id=0, has_side_effects=True, vmem_limit_bytes=56 * 2**20
        ),
        cost_estimate=pl.CostEstimate(
            flops=10 * rows * LANES * RANK, bytes_accessed=6 * rows * LANES,
            transcendentals=0,
        ),
    )(gradient, error_buffer, q_start.T)
    return (new_error[None], q_factor.T)


def solution(mesh, sizes=(4, 4, 8)):
    in_specs = (P("dp", None, "fsdp"), P("dp", None, "fsdp"), P("fsdp", None))
    out_specs = (P("dp", None, "fsdp"), P("fsdp", None))
    return jax.shard_map(
        functools.partial(on_device, sizes), mesh=mesh, in_specs=in_specs,
        out_specs=out_specs, check_vma=False,
    )
```

```python
import functools

import jax
import jax.numpy as jnp
from jax import lax
from jax.experimental import pallas as pl
from jax.experimental.pallas import tpu as pltpu
from jax.sharding import PartitionSpec as P

ITERS = 2
RANK = 64
LANES = 128
SUB = 8
BATCHES = (4, 4, 3, 3)
YL = 2
ORDER = (
    (0, 0), (0, 1), (1, 0), (0, 2), (1, 1), (0, 3),
    (2, 0), (1, 2), (2, 1), (1, 3), (3, 0), (2, 2),
    (3, 1), (2, 3), (4, 0), (3, 2), (4, 1), (3, 3),
    (5, 0), (4, 2), (5, 1), (4, 3), (6, 0), (5, 2),
    (6, 1), (5, 3), (7, 0), (6, 2), (7, 1), (6, 3),
    (8, 0), (7, 2), (8, 1), (7, 3), (8, 2), (8, 3),
)
MESH = pl.DeviceIdType.MESH
HIGHEST = lax.Precision.HIGHEST
F32 = jnp.float32
BF16 = jnp.bfloat16


def split3(value):
    hi = value.astype(BF16)
    rest = value - hi.astype(F32)
    mid = rest.astype(BF16)
    lo = (rest - mid.astype(F32)).astype(BF16)
    return hi, mid, lo


def dot(a, b, dims, precision=None):
    return lax.dot_general(
        a, b, (dims, ((), ())), precision=precision, preferred_element_type=F32
    )


def inverse_factor(gram):
    rank = gram.shape[0]
    rows = lax.broadcasted_iota(jnp.int32, (rank, rank), 0)
    cols = lax.broadcasted_iota(jnp.int32, (rank, rank), 1)
    eye = (rows == cols).astype(F32)
    work = jnp.concatenate([gram, eye], axis=1)
    below = lax.broadcasted_iota(jnp.int32, (rank, 1), 0)
    done = []
    for k in range(rank):
        first = (k // SUB) * SUB
        row = work[k - first : k - first + 1, :]
        factor = work[:, k : k + 1] / row[:, k : k + 1]
        factor = jnp.where(below[first:] > k, factor, 0.0)
        work = work - factor * row
        if k % SUB == SUB - 1:
            done.append(work[:SUB])
            work = work[SUB:]
    work = jnp.concatenate(done, axis=0)
    pivots = jnp.sum(work[:, :rank] * eye, axis=1, keepdims=True)
    return work[:, rank:] / jnp.sqrt(pivots)


def padded(per, zhalf):
    return -(-per // zhalf) * zhalf


def kernel(sizes, g_hbm, e_hbm, q_ref, out_hbm, qn_ref, w_ref,
           g_ref, e_ref, turned, rq, acc, gacc, qt, load, store, send, recv, *held):
    nx, ny, nz = sizes
    jcs = nx * ny // 2
    zhalf = nz // 2
    dp = lax.axis_index("dp")
    fs = lax.axis_index("fsdp")
    x = lax.rem(dp, nx)
    ylo = dp // nx
    yh = ny // YL
    core = lax.rem(fs, 2)
    yhi = lax.rem(fs // 2, yh)
    z = fs // (2 * yh)
    y = yhi * YL + ylo
    other = lax.rem(core + 1, 2)
    replicas = YL * nx
    count = len(BATCHES)
    starts = [sum(BATCHES[:b]) * jcs * LANES for b in range(count)]
    sizes_of = [per * jcs * LANES for per in BATCHES]
    p, o, r0, r1a, r1b, r2a, r2b, r3 = (
        held[n * count : (n + 1) * count] for n in range(8)
    )

    loads = []
    for b in range(count):
        rows = pl.ds(starts[b], sizes_of[b])
        for n, (src, dst) in enumerate(((g_hbm, g_ref), (e_hbm, e_ref))):
            copy = pltpu.make_async_copy(src.at[rows], dst.at[rows], load.at[2 * b + n])
            copy.start()
            loads.append(copy)

    def device(dx, dy, dz, dc):
        tx = lax.rem(x + dx, nx)
        ty = lax.rem(y + dy, ny)
        tz = lax.rem(z + dz, nz)
        tc = lax.rem(core + dc, 2)
        return (lax.rem(ty, YL) * nx + tx, (tz * yh + ty // YL) * 2 + tc)

    def replica(d):
        return (lax.rem(dp + d, replicas), fs)

    peers = [device(0, 0, 0, 1)]
    peers += [device(d, 0, 0, 0) for d in range(1, nx)]
    peers += [device(0, d, 0, 0) for d in range(1, ny)]
    peers += [device(0, 0, d, 0) for d in range(1, nz)]
    peers += [
        (lax.rem(ylo + 1, YL) * nx + lax.rem(x + d, nx), fs) for d in range(1, nx)
    ]
    barrier = pltpu.get_barrier_semaphore()
    for peer in peers:
        pl.semaphore_signal(barrier, inc=1, device_id=peer, device_id_type=MESH)

    qt[...] = q_ref[...]
    for b, per in enumerate(BATCHES):
        pad = padded(per, zhalf) - per
        if pad:
            p[b][:, :, :, :, per:] = jnp.zeros((2, 2, 2, jcs, pad, SUB, LANES), F32)
    pl.semaphore_wait(barrier, len(peers))

    def at(index):
        return index // jcs, lax.rem(index, jcs)

    mine = (at(x * ny + y), at(y * nx + x))

    def both(b, start, size):
        rows = pl.ds(pl.multiple_of(starts[b] + start, LANES), size)
        return jnp.concatenate([g_ref[rows, :], e_ref[rows, :]], axis=1)

    def z_block(ref, b, zz):
        part = zz // zhalf
        hi = part * mine[1][0] + (1 - part) * mine[0][0]
        jc = part * mine[1][1] + (1 - part) * mine[0][1]
        zt = padded(BATCHES[b], zhalf) // zhalf
        return ref[b].at[core, part, hi, jc, pl.ds(lax.rem(zz, zhalf) * zt, zt)]

    def row_of(ref, b, part, chip):
        hi, jc = at(chip * (ny, nx)[part])
        used = pl.ds(0, BATCHES[b])
        return ref[b].at[core, part, hi, pl.ds(jc, (ny, nx)[part]), used]

    def one_of(ref, b, part, index):
        hi, jc = at(index)
        return ref[b].at[core, part, hi, jc, pl.ds(0, BATCHES[b])]

    def out_copy(b):
        rows = pl.ds(starts[b], sizes_of[b])
        return pltpu.make_async_copy(turned.at[rows], out_hbm.at[rows], store.at[b])

    def one_iteration(it, carry):
        issued = [0]

        def push(src, dst, target):
            n = issued[0]
            issued[0] += 1
            copy = pltpu.make_async_remote_copy(
                src_ref=src, dst_ref=dst, send_sem=send.at[n], recv_sem=recv.at[n],
                device_id=target, device_id_type=MESH,
            )
            copy.start()
            return copy

        def finish(copies):
            for copy in copies:
                copy.wait()

        parts = split3(qt[...])
        left = jnp.concatenate(
            [jnp.concatenate([v, v], axis=1) for v in parts], axis=0
        )

        def project(b):
            per = BATCHES[b]
            wide = 2 * per * LANES

            def step(k, c):
                out = dot(left, both(b, k * wide, wide), ((1,), (1,)))
                out = out[:RANK] + out[RANK : 2 * RANK] + out[2 * RANK :]
                for j in range(2 * per):
                    tile = out[:, j * LANES : (j + 1) * LANES]
                    p[b][:, :, :, 2 * k + j // per, j % per] = tile.reshape(
                        2, 2, 2, SUB, LANES
                    )
                return c

            lax.fori_loop(0, jcs // 2, step, 0)

        def core_send(b):
            src = p[b].at[other, :, :, :, pl.ds(0, BATCHES[b])]
            return [push(src, r0[b], device(0, 0, 0, 1))]

        def core_add(b):
            def step(jc, c):
                p[b][core, :, :, jc, : BATCHES[b]] += r0[b][:, :, jc]
                return c

            lax.fori_loop(0, jcs, step, 0)

        def first_send(b):
            copies = []
            for d in range(1, max(nx, ny)):
                if d < nx:
                    src = row_of(p, b, 0, lax.rem(x + d, nx))
                    copies.append(push(src, r1a[b].at[d - 1], device(d, 0, 0, 0)))
                if d < ny:
                    src = row_of(p, b, 1, lax.rem(y + d, ny))
                    copies.append(push(src, r1b[b].at[d - 1], device(0, d, 0, 0)))
            return copies

        def first_add(b):
            for part, chip, got, peers in ((0, x, r1a, nx - 1), (1, y, r1b, ny - 1)):
                target = row_of(p, b, part, chip)
                total = target[...]
                for d in range(peers):
                    total = total + got[b][d]
                target[...] = total

        def second_send(b):
            copies = []
            for d in range(1, max(nx, ny)):
                if d < ny:
                    src = one_of(p, b, 0, x * ny + lax.rem(y + d, ny))
                    copies.append(push(src, r2a[b].at[d - 1], device(0, d, 0, 0)))
                if d < nx:
                    src = one_of(p, b, 1, y * nx + lax.rem(x + d, nx))
                    copies.append(push(src, r2b[b].at[d - 1], device(d, 0, 0, 0)))
            return copies

        def second_add(b):
            for part, got, peers in ((0, r2a, ny - 1), (1, r2b, nx - 1)):
                target = one_of(p, b, part, (x * ny + y, y * nx + x)[part])
                total = target[...]
                for d in range(peers):
                    total = total + got[b][d]
                target[...] = total

        def z_send(b):
            copies = []
            for d in range(1, nz):
                src = z_block(p, b, lax.rem(z + d, nz))
                copies.append(push(src, r3[b].at[d - 1], device(0, 0, d, 0)))
            return copies

        def z_add(b):
            total = z_block(p, b, z)[...]
            for d in range(nz - 1):
                total = total + r3[b][d]
            z_block(o, b, z)[...] = total

        def z_spread(b):
            block = z_block(o, b, z)
            return [push(block, block, device(0, 0, d, 0)) for d in range(1, nz)]

        def second_spread(b):
            copies = []
            one = [one_of(o, b, 0, x * ny + y), one_of(o, b, 1, y * nx + x)]
            for d in range(1, max(nx, ny)):
                if d < ny:
                    copies.append(push(one[0], one[0], device(0, d, 0, 0)))
                if d < nx:
                    copies.append(push(one[1], one[1], device(d, 0, 0, 0)))
            return copies

        def first_spread(b):
            copies = []
            row = [row_of(o, b, 0, x), row_of(o, b, 1, y)]
            for d in range(1, max(nx, ny)):
                if d < nx:
                    copies.append(push(row[0], row[0], device(d, 0, 0, 0)))
                if d < ny:
                    copies.append(push(row[1], row[1], device(0, d, 0, 0)))
            return copies

        def core_spread(b):
            block = o[b].at[core, :, :, :, pl.ds(0, BATCHES[b])]
            return [push(block, block, device(0, 0, 0, 1))]

        def tiles_of(b, jc):
            return [
                o[b][:, :, :, jc, s].reshape(RANK, LANES) for s in range(BATCHES[b])
            ]

        def back(b):
            tiles = []
            for jc in range(jcs):
                tiles += tiles_of(b, jc)
            stack = jnp.concatenate(split3(jnp.concatenate(tiles, axis=1)), axis=0)
            acc[...] += dot(stack, both(b, 0, sizes_of[b]), ((1,), (0,)))
            gacc[...] += dot(stack, stack, ((1,), (1,)))

        def turn(b):
            @pl.when(it == ITERS - 1)
            def _():
                def step(jc, c):
                    for s, tile in enumerate(tiles_of(b, jc)):
                        hi = tile.astype(BF16).astype(F32)
                        pair = jnp.concatenate([hi, tile - hi], axis=0)
                        start = starts[b] + (jc * BATCHES[b] + s) * LANES
                        rows = pl.ds(pl.multiple_of(start, LANES), LANES)
                        turned[rows, :] = pair.T.astype(BF16)
                    return c

                lax.fori_loop(0, jcs, step, 0)
                out_copy(b).start()

        def loaded(b):
            @pl.when(it == 0)
            def _():
                loads[2 * b].wait()
                loads[2 * b + 1].wait()

        acc[...] = jnp.zeros_like(acc)
        gacc[...] = jnp.zeros_like(gacc)
        flying = [None] * count

        def enter(b):
            loaded(b)
            project(b)

        def leave(b):
            back(b)
            if b < count - 1:
                turn(b)

        stages = (
            (enter, core_send),
            (core_add, first_send),
            (first_add, second_send),
            (second_add, z_send),
            (z_add, z_spread),
            (None, second_spread),
            (None, first_spread),
            (None, core_spread),
            (leave, None),
        )
        for step, b in ORDER:
            work, start = stages[step]
            if step:
                finish(flying[b])
            if work is not None:
                work(b)
            if start is not None:
                flying[b] = start(b)

        right = acc[...]
        right = right[:, :LANES] + right[:, LANES:]
        right = right[:RANK] + right[RANK : 2 * RANK] + right[2 * RANK :]
        rq[dp] = right
        copies = [push(rq.at[dp], rq.at[dp], replica(d)) for d in range(1, replicas)]
        gram = gacc[...]
        gram = gram[:, :RANK] + gram[:, RANK : 2 * RANK] + gram[:, 2 * RANK :]
        gram = gram[:RANK] + gram[RANK : 2 * RANK] + gram[2 * RANK :]
        inverse = inverse_factor(gram / (replicas * replicas))
        turn(count - 1)
        finish(copies)
        right = rq[0]
        for d in range(1, replicas):
            right = right + rq[d]
        right = right / (replicas * replicas)
        q_next = dot(inverse, right, ((1,), (0,)), HIGHEST)
        qt[...] = q_next

        @pl.when(it == ITERS - 1)
        def _():
            qn_ref[...] = q_next
            w_ref[...] = dot(inverse, q_next, ((0,), (0,)), HIGHEST) / replicas

        return carry

    lax.fori_loop(0, ITERS, one_iteration, 0)
    for b in range(count):
        out_copy(b).wait()


def finish_kernel(steps, turned_hbm, q_ref, w_ref, g_hbm, e_hbm, out_hbm, qn_ref,
                  turned, g_ref, e_ref, result, load, store):
    span = result.shape[0] // steps

    def fetch(k):
        rows = pl.ds(pl.multiple_of(k * span, span), span)
        pairs = ((turned_hbm, turned), (g_hbm, g_ref), (e_hbm, e_ref))
        return [
            pltpu.make_async_copy(src.at[rows], dst.at[rows], load.at[n, k])
            for n, (src, dst) in enumerate(pairs)
        ]

    def stored(k):
        rows = pl.ds(pl.multiple_of(k * span, span), span)
        return pltpu.make_async_copy(result.at[rows], out_hbm.at[rows], store.at[k])

    for k in range(steps):
        for copy in fetch(k):
            copy.start()
    hi, mid, _ = split3(w_ref[...])
    right = jnp.concatenate([hi, hi, mid, jnp.zeros_like(hi)], axis=0)
    qn_ref[...] = q_ref[...]

    def subtract(k, c):
        for copy in fetch(k):
            copy.wait()
        rows = pl.ds(pl.multiple_of(k * span, span), span)
        left = turned[rows, :]
        update = dot(jnp.concatenate([left, left], axis=1), right, ((1,), (0,)))
        accum = g_ref[rows, :].astype(F32) + e_ref[rows, :].astype(F32)
        result[rows, :] = (accum - update).astype(BF16)
        stored(k).start()
        return c

    lax.fori_loop(0, steps, subtract, 0)
    for k in range(steps):
        stored(k).wait()


def on_device(sizes, gradient, error_buffer, q_start):
    nx, ny, nz = sizes
    jcs = nx * ny // 2
    zhalf = nz // 2
    replicas = YL * nx
    count = len(BATCHES)
    per_batch = 2 + 4 * (nx - 1) + 4 * (ny - 1) + 2 * (nz - 1)
    copies = count * per_batch + replicas - 1
    vmem = pl.BlockSpec(memory_space=pltpu.VMEM)
    hbm = pl.BlockSpec(memory_space=pl.ANY)
    tile = (SUB, LANES)
    gradient, error_buffer = gradient[0], error_buffer[0]
    rows = gradient.shape[0]
    whole = pltpu.VMEM((rows, LANES), BF16)
    slots = [padded(per, zhalf) for per in BATCHES]
    held = [pltpu.VMEM((2, 2, 2, jcs, s) + tile, F32) for s in slots] * 2
    held += [pltpu.VMEM((2, 2, jcs, s) + tile, F32) for s in BATCHES]
    held += [pltpu.VMEM((nx - 1, ny, s) + tile, F32) for s in BATCHES]
    held += [pltpu.VMEM((ny - 1, nx, s) + tile, F32) for s in BATCHES]
    held += [pltpu.VMEM((ny - 1, s) + tile, F32) for s in BATCHES]
    held += [pltpu.VMEM((nx - 1, s) + tile, F32) for s in BATCHES]
    held += [pltpu.VMEM((nz - 1, s // zhalf) + tile, F32) for s in slots]
    small = jax.ShapeDtypeStruct((RANK, LANES), F32)
    turned, q_last, weight = pl.pallas_call(
        functools.partial(kernel, sizes),
        out_shape=(jax.ShapeDtypeStruct(gradient.shape, BF16), small, small),
        in_specs=[hbm, hbm, vmem],
        out_specs=(hbm, vmem, vmem),
        scratch_shapes=[
            whole,
            whole,
            whole,
            pltpu.VMEM((replicas, RANK, LANES), F32),
            pltpu.VMEM((3 * RANK, 2 * LANES), F32),
            pltpu.VMEM((3 * RANK, 3 * RANK), F32),
            pltpu.VMEM((RANK, LANES), F32),
            pltpu.SemaphoreType.DMA((2 * count,)),
            pltpu.SemaphoreType.DMA((count,)),
            pltpu.SemaphoreType.DMA((copies,)),
            pltpu.SemaphoreType.DMA((copies,)),
        ] + held,
        compiler_params=pltpu.CompilerParams(
            collective_id=0, has_side_effects=True, vmem_limit_bytes=56 * 2**20
        ),
        cost_estimate=pl.CostEstimate(
            flops=8 * rows * LANES * RANK, bytes_accessed=6 * rows * LANES,
            transcendentals=0,
        ),
    )(gradient, error_buffer, q_start.T)
    steps = jcs
    new_error, q_factor = pl.pallas_call(
        functools.partial(finish_kernel, steps),
        out_shape=(jax.ShapeDtypeStruct(gradient.shape, BF16), small),
        in_specs=[hbm, vmem, vmem, hbm, hbm],
        out_specs=(hbm, vmem),
        scratch_shapes=[whole] * 4 + [
            pltpu.SemaphoreType.DMA((3, steps)),
            pltpu.SemaphoreType.DMA((steps,)),
        ],
        compiler_params=pltpu.CompilerParams(vmem_limit_bytes=56 * 2**20),
        cost_estimate=pl.CostEstimate(
            flops=2 * rows * LANES * RANK, bytes_accessed=8 * rows * LANES,
            transcendentals=0,
        ),
    )(turned, q_last, weight, gradient, error_buffer)
    return (new_error[None], q_factor.T)


def solution(mesh, sizes=(4, 4, 8)):
    in_specs = (P("dp", None, "fsdp"), P("dp", None, "fsdp"), P("fsdp", None))
    out_specs = (P("dp", None, "fsdp"), P("fsdp", None))
    return jax.shard_map(
        functools.partial(on_device, sizes), mesh=mesh, in_specs=in_specs,
        out_specs=out_specs, check_vma=False,
    )
```

```python
import functools

import jax
import jax.numpy as jnp
from jax import lax
from jax.experimental import pallas as pl
from jax.experimental.pallas import tpu as pltpu
from jax.sharding import PartitionSpec as P

ITERS = 2
RANK = 64
LANES = 128
SUB = 8
BATCHES = (4, 4, 3, 3)
YL = 2
ORDER = (
    (0, 0), (0, 1), (1, 0), (0, 2), (1, 1), (0, 3),
    (2, 0), (1, 2), (2, 1), (1, 3), (3, 0), (2, 2),
    (3, 1), (2, 3), (4, 0), (3, 2), (4, 1), (3, 3),
    (5, 0), (4, 2), (5, 1), (4, 3), (6, 0), (5, 2),
    (6, 1), (5, 3), (7, 0), (6, 2), (7, 1), (6, 3),
    (8, 0), (7, 2), (8, 1), (7, 3), (8, 2), (8, 3),
)
MESH = pl.DeviceIdType.MESH
HIGHEST = lax.Precision.HIGHEST
F32 = jnp.float32
BF16 = jnp.bfloat16


def split3(value):
    hi = value.astype(BF16)
    rest = value - hi.astype(F32)
    mid = rest.astype(BF16)
    lo = (rest - mid.astype(F32)).astype(BF16)
    return hi, mid, lo


def dot(a, b, dims, precision=None):
    return lax.dot_general(
        a, b, (dims, ((), ())), precision=precision, preferred_element_type=F32
    )


def inverse_factor(gram):
    rank = gram.shape[0]
    rows = lax.broadcasted_iota(jnp.int32, (rank, rank), 0)
    cols = lax.broadcasted_iota(jnp.int32, (rank, rank), 1)
    eye = (rows == cols).astype(F32)
    work = jnp.concatenate([gram, eye], axis=1)
    below = lax.broadcasted_iota(jnp.int32, (rank, 1), 0)
    done = []
    for k in range(rank):
        first = (k // SUB) * SUB
        row = work[k - first : k - first + 1, :]
        factor = work[:, k : k + 1] / row[:, k : k + 1]
        factor = jnp.where(below[first:] > k, factor, 0.0)
        work = work - factor * row
        if k % SUB == SUB - 1:
            done.append(work[:SUB])
            work = work[SUB:]
    work = jnp.concatenate(done, axis=0)
    pivots = jnp.sum(work[:, :rank] * eye, axis=1, keepdims=True)
    return work[:, rank:] / jnp.sqrt(pivots)


def padded(per, zhalf):
    return -(-per // zhalf) * zhalf


def kernel(sizes, g_hbm, e_hbm, q_hbm, out_ref, qn_ref,
           g_ref, e_ref, turned, rq, acc, gacc, qt, weight, load, send, recv, *held):
    nx, ny, nz = sizes
    jcs = nx * ny // 2
    zhalf = nz // 2
    dp = lax.axis_index("dp")
    fs = lax.axis_index("fsdp")
    x = lax.rem(dp, nx)
    ylo = dp // nx
    yh = ny // YL
    core = lax.rem(fs, 2)
    yhi = lax.rem(fs // 2, yh)
    z = fs // (2 * yh)
    y = yhi * YL + ylo
    other = lax.rem(core + 1, 2)
    replicas = YL * nx
    count = len(BATCHES)
    starts = [sum(BATCHES[:b]) * jcs * LANES for b in range(count)]
    sizes_of = [per * jcs * LANES for per in BATCHES]
    p, o, r0, r1a, r1b, r2a, r2b, r3 = (
        held[n * count : (n + 1) * count] for n in range(8)
    )

    first_q = pltpu.make_async_copy(q_hbm, qt, load.at[2 * count])
    first_q.start()
    loads = []
    for b in range(count):
        rows = pl.ds(starts[b], sizes_of[b])
        for n, (src, dst) in enumerate(((g_hbm, g_ref), (e_hbm, e_ref))):
            copy = pltpu.make_async_copy(src.at[rows], dst.at[rows], load.at[2 * b + n])
            copy.start()
            loads.append(copy)

    def device(dx, dy, dz, dc):
        tx = lax.rem(x + dx, nx)
        ty = lax.rem(y + dy, ny)
        tz = lax.rem(z + dz, nz)
        tc = lax.rem(core + dc, 2)
        return (lax.rem(ty, YL) * nx + tx, (tz * yh + ty // YL) * 2 + tc)

    def replica(d):
        return (lax.rem(dp + d, replicas), fs)

    peers = [device(0, 0, 0, 1)]
    peers += [device(d, 0, 0, 0) for d in range(1, nx)]
    peers += [device(0, d, 0, 0) for d in range(1, ny)]
    peers += [device(0, 0, d, 0) for d in range(1, nz)]
    peers += [
        (lax.rem(ylo + 1, YL) * nx + lax.rem(x + d, nx), fs) for d in range(1, nx)
    ]
    barrier = pltpu.get_barrier_semaphore()
    for peer in peers:
        pl.semaphore_signal(barrier, inc=1, device_id=peer, device_id_type=MESH)

    for b, per in enumerate(BATCHES):
        pad = padded(per, zhalf) - per
        if pad:
            p[b][:, :, :, :, per:] = jnp.zeros((2, 2, 2, jcs, pad, SUB, LANES), F32)
    first_q.wait()
    pl.semaphore_wait(barrier, len(peers))

    def at(index):
        return index // jcs, lax.rem(index, jcs)

    mine = (at(x * ny + y), at(y * nx + x))

    def both(b, start, size):
        rows = pl.ds(pl.multiple_of(starts[b] + start, LANES), size)
        return jnp.concatenate([g_ref[rows, :], e_ref[rows, :]], axis=1)

    def z_block(ref, b, zz):
        part = zz // zhalf
        hi = part * mine[1][0] + (1 - part) * mine[0][0]
        jc = part * mine[1][1] + (1 - part) * mine[0][1]
        zt = padded(BATCHES[b], zhalf) // zhalf
        return ref[b].at[core, part, hi, jc, pl.ds(lax.rem(zz, zhalf) * zt, zt)]

    def row_of(ref, b, part, chip):
        hi, jc = at(chip * (ny, nx)[part])
        used = pl.ds(0, BATCHES[b])
        return ref[b].at[core, part, hi, pl.ds(jc, (ny, nx)[part]), used]

    def one_of(ref, b, part, index):
        hi, jc = at(index)
        return ref[b].at[core, part, hi, jc, pl.ds(0, BATCHES[b])]

    def one_iteration(it, carry):
        issued = [0]

        def push(src, dst, target):
            n = issued[0]
            issued[0] += 1
            copy = pltpu.make_async_remote_copy(
                src_ref=src, dst_ref=dst, send_sem=send.at[n], recv_sem=recv.at[n],
                device_id=target, device_id_type=MESH,
            )
            copy.start()
            return copy

        def finish(copies):
            for copy in copies:
                copy.wait()

        parts = split3(qt[...])
        left = jnp.concatenate(
            [jnp.concatenate([v, v], axis=1) for v in parts], axis=0
        )

        def project(b):
            per = BATCHES[b]
            wide = 2 * per * LANES

            def step(k, c):
                out = dot(left, both(b, k * wide, wide), ((1,), (1,)))
                out = out[:RANK] + out[RANK : 2 * RANK] + out[2 * RANK :]
                for j in range(2 * per):
                    tile = out[:, j * LANES : (j + 1) * LANES]
                    p[b][:, :, :, 2 * k + j // per, j % per] = tile.reshape(
                        2, 2, 2, SUB, LANES
                    )
                return c

            lax.fori_loop(0, jcs // 2, step, 0)

        def core_send(b):
            src = p[b].at[other, :, :, :, pl.ds(0, BATCHES[b])]
            return [push(src, r0[b], device(0, 0, 0, 1))]

        def core_add(b):
            def step(jc, c):
                p[b][core, :, :, jc, : BATCHES[b]] += r0[b][:, :, jc]
                return c

            lax.fori_loop(0, jcs, step, 0)

        def first_send(b):
            copies = []
            for d in range(1, max(nx, ny)):
                if d < nx:
                    src = row_of(p, b, 0, lax.rem(x + d, nx))
                    copies.append(push(src, r1a[b].at[d - 1], device(d, 0, 0, 0)))
                if d < ny:
                    src = row_of(p, b, 1, lax.rem(y + d, ny))
                    copies.append(push(src, r1b[b].at[d - 1], device(0, d, 0, 0)))
            return copies

        def first_add(b):
            for part, chip, got, peers in ((0, x, r1a, nx - 1), (1, y, r1b, ny - 1)):
                target = row_of(p, b, part, chip)
                total = target[...]
                for d in range(peers):
                    total = total + got[b][d]
                target[...] = total

        def second_send(b):
            copies = []
            for d in range(1, max(nx, ny)):
                if d < ny:
                    src = one_of(p, b, 0, x * ny + lax.rem(y + d, ny))
                    copies.append(push(src, r2a[b].at[d - 1], device(0, d, 0, 0)))
                if d < nx:
                    src = one_of(p, b, 1, y * nx + lax.rem(x + d, nx))
                    copies.append(push(src, r2b[b].at[d - 1], device(d, 0, 0, 0)))
            return copies

        def second_add(b):
            for part, got, peers in ((0, r2a, ny - 1), (1, r2b, nx - 1)):
                target = one_of(p, b, part, (x * ny + y, y * nx + x)[part])
                total = target[...]
                for d in range(peers):
                    total = total + got[b][d]
                target[...] = total

        def z_send(b):
            copies = []
            for d in range(1, nz):
                src = z_block(p, b, lax.rem(z + d, nz))
                copies.append(push(src, r3[b].at[d - 1], device(0, 0, d, 0)))
            return copies

        def z_add(b):
            total = z_block(p, b, z)[...]
            for d in range(nz - 1):
                total = total + r3[b][d]
            z_block(o, b, z)[...] = total

        def z_spread(b):
            block = z_block(o, b, z)
            return [push(block, block, device(0, 0, d, 0)) for d in range(1, nz)]

        def second_spread(b):
            copies = []
            one = [one_of(o, b, 0, x * ny + y), one_of(o, b, 1, y * nx + x)]
            for d in range(1, max(nx, ny)):
                if d < ny:
                    copies.append(push(one[0], one[0], device(0, d, 0, 0)))
                if d < nx:
                    copies.append(push(one[1], one[1], device(d, 0, 0, 0)))
            return copies

        def first_spread(b):
            copies = []
            row = [row_of(o, b, 0, x), row_of(o, b, 1, y)]
            for d in range(1, max(nx, ny)):
                if d < nx:
                    copies.append(push(row[0], row[0], device(d, 0, 0, 0)))
                if d < ny:
                    copies.append(push(row[1], row[1], device(0, d, 0, 0)))
            return copies

        def core_spread(b):
            block = o[b].at[core, :, :, :, pl.ds(0, BATCHES[b])]
            return [push(block, block, device(0, 0, 0, 1))]

        def tiles_of(b, jc):
            return [
                o[b][:, :, :, jc, s].reshape(RANK, LANES) for s in range(BATCHES[b])
            ]

        def back(b):
            tiles = []
            for jc in range(jcs):
                tiles += tiles_of(b, jc)
            stack = jnp.concatenate(split3(jnp.concatenate(tiles, axis=1)), axis=0)
            acc[...] += dot(stack, both(b, 0, sizes_of[b]), ((1,), (0,)))
            gacc[...] += dot(stack, stack, ((1,), (1,)))

        def turn(b):
            @pl.when(it == ITERS - 1)
            def _():
                def step(jc, c):
                    for s, tile in enumerate(tiles_of(b, jc)):
                        hi = tile.astype(BF16).astype(F32)
                        pair = jnp.concatenate([hi, tile - hi], axis=0)
                        start = starts[b] + (jc * BATCHES[b] + s) * LANES
                        rows = pl.ds(pl.multiple_of(start, LANES), LANES)
                        turned[rows, :] = pair.T.astype(BF16)
                    return c

                lax.fori_loop(0, jcs, step, 0)

        def loaded(b):
            @pl.when(it == 0)
            def _():
                loads[2 * b].wait()
                loads[2 * b + 1].wait()

        acc[...] = jnp.zeros_like(acc)
        gacc[...] = jnp.zeros_like(gacc)
        flying = [None] * count

        def enter(b):
            loaded(b)
            project(b)

        def leave(b):
            back(b)
            if b < count - 1:
                turn(b)

        stages = (
            (enter, core_send),
            (core_add, first_send),
            (first_add, second_send),
            (second_add, z_send),
            (z_add, z_spread),
            (None, second_spread),
            (None, first_spread),
            (None, core_spread),
            (leave, None),
        )
        for step, b in ORDER:
            work, start = stages[step]
            if step:
                finish(flying[b])
            if work is not None:
                work(b)
            if start is not None:
                flying[b] = start(b)

        right = acc[...]
        right = right[:, :LANES] + right[:, LANES:]
        right = right[:RANK] + right[RANK : 2 * RANK] + right[2 * RANK :]
        rq[dp] = right
        copies = [push(rq.at[dp], rq.at[dp], replica(d)) for d in range(1, replicas)]
        gram = gacc[...]
        gram = gram[:, :RANK] + gram[:, RANK : 2 * RANK] + gram[:, 2 * RANK :]
        gram = gram[:RANK] + gram[RANK : 2 * RANK] + gram[2 * RANK :]
        inverse = inverse_factor(gram / (replicas * replicas))
        turn(count - 1)
        finish(copies)
        right = rq[0]
        for d in range(1, replicas):
            right = right + rq[d]
        right = right / (replicas * replicas)
        q_next = dot(inverse, right, ((1,), (0,)), HIGHEST)
        qt[...] = q_next

        @pl.when(it == ITERS - 1)
        def _():
            qn_ref[...] = q_next
            weight[...] = dot(inverse, q_next, ((0,), (0,)), HIGHEST) / replicas

        return carry

    lax.fori_loop(0, ITERS, one_iteration, 0)
    hi, mid, _ = split3(weight[...])
    right = jnp.concatenate([hi, hi, mid, jnp.zeros_like(hi)], axis=0)
    span = 2 * sum(BATCHES) * LANES

    def subtract(k, c):
        rows = pl.ds(pl.multiple_of(k * span, span), span)
        left = turned[rows, :]
        update = dot(jnp.concatenate([left, left], axis=1), right, ((1,), (0,)))
        accum = g_ref[rows, :].astype(F32) + e_ref[rows, :].astype(F32)
        out_ref[rows, :] = (accum - update).astype(BF16)
        return c

    lax.fori_loop(0, jcs // 2, subtract, 0)


def on_device(sizes, gradient, error_buffer, q_start):
    nx, ny, nz = sizes
    jcs = nx * ny // 2
    zhalf = nz // 2
    replicas = YL * nx
    count = len(BATCHES)
    per_batch = 2 + 4 * (nx - 1) + 4 * (ny - 1) + 2 * (nz - 1)
    copies = count * per_batch + replicas - 1
    vmem = pl.BlockSpec(memory_space=pltpu.VMEM)
    hbm = pl.BlockSpec(memory_space=pltpu.HBM)
    tile = (SUB, LANES)
    gradient, error_buffer = gradient[0], error_buffer[0]
    rows = gradient.shape[0]
    whole = pltpu.VMEM((rows, LANES), BF16)
    slots = [padded(per, zhalf) for per in BATCHES]
    held = [pltpu.VMEM((2, 2, 2, jcs, s) + tile, F32) for s in slots] * 2
    held += [pltpu.VMEM((2, 2, jcs, s) + tile, F32) for s in BATCHES]
    held += [pltpu.VMEM((nx - 1, ny, s) + tile, F32) for s in BATCHES]
    held += [pltpu.VMEM((ny - 1, nx, s) + tile, F32) for s in BATCHES]
    held += [pltpu.VMEM((ny - 1, s) + tile, F32) for s in BATCHES]
    held += [pltpu.VMEM((nx - 1, s) + tile, F32) for s in BATCHES]
    held += [pltpu.VMEM((nz - 1, s // zhalf) + tile, F32) for s in slots]
    small = jax.ShapeDtypeStruct((RANK, LANES), F32)
    new_error, q_factor = pl.pallas_call(
        functools.partial(kernel, sizes),
        out_shape=(jax.ShapeDtypeStruct(gradient.shape, BF16), small),
        in_specs=[hbm] * 3,
        out_specs=(vmem, vmem),
        scratch_shapes=[
            whole,
            whole,
            whole,
            pltpu.VMEM((replicas, RANK, LANES), F32),
            pltpu.VMEM((3 * RANK, 2 * LANES), F32),
            pltpu.VMEM((3 * RANK, 3 * RANK), F32),
            pltpu.VMEM((RANK, LANES), F32),
            pltpu.VMEM((RANK, LANES), F32),
            pltpu.SemaphoreType.DMA((2 * count + 1,)),
            pltpu.SemaphoreType.DMA((copies,)),
            pltpu.SemaphoreType.DMA((copies,)),
        ] + held,
        compiler_params=pltpu.CompilerParams(
            collective_id=0, has_side_effects=True, vmem_limit_bytes=40 * 2**20
        ),
        cost_estimate=pl.CostEstimate(
            flops=8 * rows * LANES * RANK, bytes_accessed=6 * rows * LANES,
            transcendentals=0,
        ),
    )(*[
        pltpu.with_memory_space_constraint(value, pltpu.HBM)
        for value in (gradient, error_buffer, q_start.T)
    ])
    return (new_error[None], q_factor.T)


def solution(mesh, sizes=(4, 4, 8)):
    in_specs = (P("dp", None, "fsdp"), P("dp", None, "fsdp"), P("fsdp", None))
    out_specs = (P("dp", None, "fsdp"), P("fsdp", None))
    return jax.shard_map(
        functools.partial(on_device, sizes), mesh=mesh, in_specs=in_specs,
        out_specs=out_specs, check_vma=False,
    )
```

```python
import functools

import jax
import jax.numpy as jnp
from jax import lax
from jax.experimental import pallas as pl
from jax.experimental.pallas import tpu as pltpu
from jax.sharding import PartitionSpec as P

ITERS = 2
RANK = 64
LANES = 128
SUB = 8
BATCHES = (4, 4, 3, 3)
YL = 2
ORDER = (
    (0, 0), (0, 1), (1, 0), (0, 2), (1, 1), (0, 3),
    (2, 0), (1, 2), (2, 1), (1, 3), (3, 0), (2, 2),
    (3, 1), (2, 3), (4, 0), (3, 2), (4, 1), (3, 3),
    (5, 0), (4, 2), (5, 1), (4, 3), (6, 0), (5, 2),
    (6, 1), (5, 3), (7, 0), (6, 2), (7, 1), (6, 3),
    (8, 0), (7, 2), (8, 1), (7, 3), (8, 2), (8, 3),
)
MESH = pl.DeviceIdType.MESH
HIGHEST = lax.Precision.HIGHEST
F32 = jnp.float32
BF16 = jnp.bfloat16


def split3(value):
    hi = value.astype(BF16)
    rest = value - hi.astype(F32)
    mid = rest.astype(BF16)
    lo = (rest - mid.astype(F32)).astype(BF16)
    return hi, mid, lo


def dot(a, b, dims, precision=None):
    return lax.dot_general(
        a, b, (dims, ((), ())), precision=precision, preferred_element_type=F32
    )


def inverse_factor(gram):
    rank = gram.shape[0]
    rows = lax.broadcasted_iota(jnp.int32, (rank, rank), 0)
    cols = lax.broadcasted_iota(jnp.int32, (rank, rank), 1)
    eye = (rows == cols).astype(F32)
    work = jnp.concatenate([gram, eye], axis=1)
    below = lax.broadcasted_iota(jnp.int32, (rank, 1), 0)
    done = []
    for k in range(rank):
        first = (k // SUB) * SUB
        row = work[k - first : k - first + 1, :]
        factor = work[:, k : k + 1] / row[:, k : k + 1]
        factor = jnp.where(below[first:] > k, factor, 0.0)
        work = work - factor * row
        if k % SUB == SUB - 1:
            done.append(work[:SUB])
            work = work[SUB:]
    work = jnp.concatenate(done, axis=0)
    pivots = jnp.sum(work[:, :rank] * eye, axis=1, keepdims=True)
    return work[:, rank:] / jnp.sqrt(pivots)


def padded(per, zhalf):
    return -(-per // zhalf) * zhalf


def kernel(sizes, g_hbm, e_hbm, q_hbm, out_ref, qn_ref,
           g_ref, e_ref, turned, rq, acc, gacc, qt, weight, load, send, recv, *held):
    nx, ny, nz = sizes
    jcs = nx * ny // 2
    zhalf = nz // 2
    dp = lax.axis_index("dp")
    fs = lax.axis_index("fsdp")
    x = lax.rem(dp, nx)
    ylo = dp // nx
    yh = ny // YL
    core = lax.rem(fs, 2)
    yhi = lax.rem(fs // 2, yh)
    z = fs // (2 * yh)
    y = yhi * YL + ylo
    other = lax.rem(core + 1, 2)
    replicas = YL * nx
    count = len(BATCHES)
    starts = [sum(BATCHES[:b]) * jcs * LANES for b in range(count)]
    sizes_of = [per * jcs * LANES for per in BATCHES]
    p, o, r0, r1a, r1b, r2a, r2b, r3 = (
        held[n * count : (n + 1) * count] for n in range(8)
    )

    first_q = pltpu.make_async_copy(q_hbm, qt, load.at[2 * count])
    first_q.start()
    loads = []
    for b in range(count):
        rows = pl.ds(starts[b], sizes_of[b])
        for n, (src, dst) in enumerate(((g_hbm, g_ref), (e_hbm, e_ref))):
            copy = pltpu.make_async_copy(src.at[rows], dst.at[rows], load.at[2 * b + n])
            copy.start()
            loads.append(copy)

    def device(dx, dy, dz, dc):
        tx = lax.rem(x + dx, nx)
        ty = lax.rem(y + dy, ny)
        tz = lax.rem(z + dz, nz)
        tc = lax.rem(core + dc, 2)
        return (lax.rem(ty, YL) * nx + tx, (tz * yh + ty // YL) * 2 + tc)

    def replica(d):
        return (lax.rem(dp + d, replicas), fs)

    peers = [device(0, 0, 0, 1)]
    peers += [device(d, 0, 0, 0) for d in range(1, nx)]
    peers += [device(0, d, 0, 0) for d in range(1, ny)]
    peers += [device(0, 0, d, 0) for d in range(1, nz)]
    peers += [
        (lax.rem(ylo + 1, YL) * nx + lax.rem(x + d, nx), fs) for d in range(1, nx)
    ]
    barrier = pltpu.get_barrier_semaphore()
    for peer in peers:
        pl.semaphore_signal(barrier, inc=1, device_id=peer, device_id_type=MESH)

    for b, per in enumerate(BATCHES):
        pad = padded(per, zhalf) - per
        if pad:
            p[b][:, :, :, :, per:] = jnp.zeros((2, 2, 2, jcs, pad, SUB, LANES), F32)
    first_q.wait()
    pl.semaphore_wait(barrier, len(peers))

    def at(index):
        return index // jcs, lax.rem(index, jcs)

    mine = (at(x * ny + y), at(y * nx + x))

    def both(b, start, size):
        rows = pl.ds(pl.multiple_of(starts[b] + start, LANES), size)
        return jnp.concatenate([g_ref[rows, :], e_ref[rows, :]], axis=1)

    def z_block(ref, b, zz):
        part = zz // zhalf
        hi = part * mine[1][0] + (1 - part) * mine[0][0]
        jc = part * mine[1][1] + (1 - part) * mine[0][1]
        zt = padded(BATCHES[b], zhalf) // zhalf
        return ref[b].at[core, part, hi, jc, pl.ds(lax.rem(zz, zhalf) * zt, zt)]

    def row_of(ref, b, part, chip):
        hi, jc = at(chip * (ny, nx)[part])
        used = pl.ds(0, BATCHES[b])
        return ref[b].at[core, part, hi, pl.ds(jc, (ny, nx)[part]), used]

    def one_of(ref, b, part, index):
        hi, jc = at(index)
        return ref[b].at[core, part, hi, jc, pl.ds(0, BATCHES[b])]

    def far_first(n):
        return sorted(range(1, n), key=lambda d: -min(d, n - d))

    def one_iteration(it, carry):
        issued = [0]

        def push(src, dst, target):
            n = issued[0]
            issued[0] += 1
            copy = pltpu.make_async_remote_copy(
                src_ref=src, dst_ref=dst, send_sem=send.at[n], recv_sem=recv.at[n],
                device_id=target, device_id_type=MESH,
            )
            copy.start()
            return copy

        def finish(copies):
            for copy in copies:
                copy.wait()

        parts = split3(qt[...])
        left = jnp.concatenate(
            [jnp.concatenate([v, v], axis=1) for v in parts], axis=0
        )

        def project(b):
            per = BATCHES[b]
            wide = 2 * per * LANES

            def step(k, c):
                out = dot(left, both(b, k * wide, wide), ((1,), (1,)))
                out = out[:RANK] + out[RANK : 2 * RANK] + out[2 * RANK :]
                for j in range(2 * per):
                    tile = out[:, j * LANES : (j + 1) * LANES]
                    p[b][:, :, :, 2 * k + j // per, j % per] = tile.reshape(
                        2, 2, 2, SUB, LANES
                    )
                return c

            lax.fori_loop(0, jcs // 2, step, 0)

        def core_send(b):
            src = p[b].at[other, :, :, :, pl.ds(0, BATCHES[b])]
            return [push(src, r0[b], device(0, 0, 0, 1))]

        def core_add(b):
            def step(jc, c):
                p[b][core, :, :, jc, : BATCHES[b]] += r0[b][:, :, jc]
                return c

            lax.fori_loop(0, jcs, step, 0)

        firsts = ((x, nx, r1a), (y, ny, r1b))
        seconds = ((y, ny, r2a), (x, nx, r2b))

        def along(part, d):
            return device(d, 0, 0, 0) if part == 0 else device(0, d, 0, 0)

        def first_send(b, part):
            chip, n, got = firsts[part]
            copies = []
            for d in far_first(n):
                src = row_of(p, b, part, lax.rem(chip + d, n))
                copies.append(push(src, got[b].at[d - 1], along(part, d)))
            return copies

        def first_add(b, part):
            chip, n, got = firsts[part]
            target = row_of(p, b, part, chip)
            total = target[...]
            for d in range(n - 1):
                total = total + got[b][d]
            target[...] = total

        def second_send(b, part):
            chip, n, got = seconds[part]
            base = (x * ny, y * nx)[part]
            copies = []
            for d in far_first(n):
                src = one_of(p, b, part, base + lax.rem(chip + d, n))
                copies.append(push(src, got[b].at[d - 1], along(1 - part, d)))
            return copies

        def second_add(b, part):
            _, n, got = seconds[part]
            target = one_of(p, b, part, (x * ny + y, y * nx + x)[part])
            total = target[...]
            for d in range(n - 1):
                total = total + got[b][d]
            target[...] = total

        def z_send(b):
            copies = []
            for d in far_first(nz):
                src = z_block(p, b, lax.rem(z + d, nz))
                copies.append(push(src, r3[b].at[d - 1], device(0, 0, d, 0)))
            return copies

        def z_add(b):
            total = z_block(p, b, z)[...]
            for d in range(nz - 1):
                total = total + r3[b][d]
            z_block(o, b, z)[...] = total

        def z_spread(b):
            block = z_block(o, b, z)
            return [push(block, block, device(0, 0, d, 0)) for d in far_first(nz)]

        def second_spread(b, part):
            block = one_of(o, b, part, (x * ny + y, y * nx + x)[part])
            n = (ny, nx)[part]
            return [push(block, block, along(1 - part, d)) for d in far_first(n)]

        def first_spread(b, part):
            chip, n, _ = firsts[part]
            block = row_of(o, b, part, chip)
            return [push(block, block, along(part, d)) for d in far_first(n)]

        def core_spread(b, part):
            block = o[b].at[core, part, :, :, pl.ds(0, BATCHES[b])]
            return [push(block, block, device(0, 0, 0, 1))]

        def tiles_of(b, jc):
            return [
                o[b][:, :, :, jc, s].reshape(RANK, LANES) for s in range(BATCHES[b])
            ]

        def back(b):
            tiles = []
            for jc in range(jcs):
                tiles += tiles_of(b, jc)
            stack = jnp.concatenate(split3(jnp.concatenate(tiles, axis=1)), axis=0)
            acc[...] += dot(stack, both(b, 0, sizes_of[b]), ((1,), (0,)))
            gacc[...] += dot(stack, stack, ((1,), (1,)))

        def turn(b):
            @pl.when(it == ITERS - 1)
            def _():
                def step(jc, c):
                    for s, tile in enumerate(tiles_of(b, jc)):
                        hi = tile.astype(BF16).astype(F32)
                        pair = jnp.concatenate([hi, tile - hi], axis=0)
                        start = starts[b] + (jc * BATCHES[b] + s) * LANES
                        rows = pl.ds(pl.multiple_of(start, LANES), LANES)
                        turned[rows, :] = pair.T.astype(BF16)
                    return c

                lax.fori_loop(0, jcs, step, 0)

        def loaded(b):
            @pl.when(it == 0)
            def _():
                loads[2 * b].wait()
                loads[2 * b + 1].wait()

        acc[...] = jnp.zeros_like(acc)
        gacc[...] = jnp.zeros_like(gacc)
        flying = [None] * count

        def enter(b):
            loaded(b)
            project(b)

        def leave(b):
            back(b)
            if b < count - 1:
                turn(b)

        stages = (
            (enter, core_send, False),
            (core_add, first_send, True),
            (first_add, second_send, True),
            (second_add, z_send, False),
            (z_add, z_spread, False),
            (None, second_spread, True),
            (None, first_spread, True),
            (None, core_spread, True),
            (leave, None, False),
        )
        for step, b in ORDER:
            work, start, by_part = stages[step]
            before = step and stages[step - 1][2]
            if before and by_part:
                for part in range(2):
                    finish(flying[b][part])
                    if work is not None:
                        work(b, part)
                    flying[b][part] = start(b, part)
                continue
            if before:
                for part in range(2):
                    finish(flying[b][part])
                    if work is second_add:
                        work(b, part)
            elif step:
                finish(flying[b])
            if work is not None and work is not second_add:
                work(b)
            if by_part:
                flying[b] = [start(b, part) for part in range(2)]
            elif start is not None:
                flying[b] = start(b)

        right = acc[...]
        right = right[:, :LANES] + right[:, LANES:]
        right = right[:RANK] + right[RANK : 2 * RANK] + right[2 * RANK :]
        rq[dp] = right
        copies = [push(rq.at[dp], rq.at[dp], replica(d)) for d in range(1, replicas)]
        gram = gacc[...]
        gram = gram[:, :RANK] + gram[:, RANK : 2 * RANK] + gram[:, 2 * RANK :]
        gram = gram[:RANK] + gram[RANK : 2 * RANK] + gram[2 * RANK :]
        inverse = inverse_factor(gram / (replicas * replicas))
        turn(count - 1)
        finish(copies)
        right = rq[0]
        for d in range(1, replicas):
            right = right + rq[d]
        right = right / (replicas * replicas)
        q_next = dot(inverse, right, ((1,), (0,)), HIGHEST)
        qt[...] = q_next

        @pl.when(it == ITERS - 1)
        def _():
            qn_ref[...] = q_next
            weight[...] = dot(inverse, q_next, ((0,), (0,)), HIGHEST) / replicas

        return carry

    lax.fori_loop(0, ITERS, one_iteration, 0)
    hi, mid, _ = split3(weight[...])
    right = jnp.concatenate([hi, hi, mid, jnp.zeros_like(hi)], axis=0)
    span = 2 * sum(BATCHES) * LANES

    def subtract(k, c):
        rows = pl.ds(pl.multiple_of(k * span, span), span)
        left = turned[rows, :]
        update = dot(jnp.concatenate([left, left], axis=1), right, ((1,), (0,)))
        accum = g_ref[rows, :].astype(F32) + e_ref[rows, :].astype(F32)
        out_ref[rows, :] = (accum - update).astype(BF16)
        return c

    lax.fori_loop(0, jcs // 2, subtract, 0)


def on_device(sizes, gradient, error_buffer, q_start):
    nx, ny, nz = sizes
    jcs = nx * ny // 2
    zhalf = nz // 2
    replicas = YL * nx
    count = len(BATCHES)
    per_batch = 3 + 4 * (nx - 1) + 4 * (ny - 1) + 2 * (nz - 1)
    copies = count * per_batch + replicas - 1
    vmem = pl.BlockSpec(memory_space=pltpu.VMEM)
    hbm = pl.BlockSpec(memory_space=pltpu.HBM)
    tile = (SUB, LANES)
    gradient, error_buffer = gradient[0], error_buffer[0]
    rows = gradient.shape[0]
    whole = pltpu.VMEM((rows, LANES), BF16)
    slots = [padded(per, zhalf) for per in BATCHES]
    held = [pltpu.VMEM((2, 2, 2, jcs, s) + tile, F32) for s in slots] * 2
    held += [pltpu.VMEM((2, 2, jcs, s) + tile, F32) for s in BATCHES]
    held += [pltpu.VMEM((nx - 1, ny, s) + tile, F32) for s in BATCHES]
    held += [pltpu.VMEM((ny - 1, nx, s) + tile, F32) for s in BATCHES]
    held += [pltpu.VMEM((ny - 1, s) + tile, F32) for s in BATCHES]
    held += [pltpu.VMEM((nx - 1, s) + tile, F32) for s in BATCHES]
    held += [pltpu.VMEM((nz - 1, s // zhalf) + tile, F32) for s in slots]
    small = jax.ShapeDtypeStruct((RANK, LANES), F32)
    new_error, q_factor = pl.pallas_call(
        functools.partial(kernel, sizes),
        out_shape=(jax.ShapeDtypeStruct(gradient.shape, BF16), small),
        in_specs=[hbm] * 3,
        out_specs=(vmem, vmem),
        scratch_shapes=[
            whole,
            whole,
            whole,
            pltpu.VMEM((replicas, RANK, LANES), F32),
            pltpu.VMEM((3 * RANK, 2 * LANES), F32),
            pltpu.VMEM((3 * RANK, 3 * RANK), F32),
            pltpu.VMEM((RANK, LANES), F32),
            pltpu.VMEM((RANK, LANES), F32),
            pltpu.SemaphoreType.DMA((2 * count + 1,)),
            pltpu.SemaphoreType.DMA((copies,)),
            pltpu.SemaphoreType.DMA((copies,)),
        ] + held,
        compiler_params=pltpu.CompilerParams(
            collective_id=0, has_side_effects=True, vmem_limit_bytes=40 * 2**20
        ),
        cost_estimate=pl.CostEstimate(
            flops=8 * rows * LANES * RANK, bytes_accessed=6 * rows * LANES,
            transcendentals=0,
        ),
    )(*[
        pltpu.with_memory_space_constraint(value, pltpu.HBM)
        for value in (gradient, error_buffer, q_start.T)
    ])
    return (new_error[None], q_factor.T)


def solution(mesh, sizes=(4, 4, 8)):
    in_specs = (P("dp", None, "fsdp"), P("dp", None, "fsdp"), P("fsdp", None))
    out_specs = (P("dp", None, "fsdp"), P("fsdp", None))
    return jax.shard_map(
        functools.partial(on_device, sizes), mesh=mesh, in_specs=in_specs,
        out_specs=out_specs, check_vma=False,
    )
```

```python
import functools

import jax
import jax.numpy as jnp
from jax import lax
from jax.experimental import pallas as pl
from jax.experimental.pallas import tpu as pltpu
from jax.sharding import PartitionSpec as P

ITERS = 2
RANK = 64
LANES = 128
SUB = 8
BATCHES = (4, 4, 4, 2)
YL = 2
ORDER = (
    (0, 0), (0, 1), (1, 0), (0, 2), (1, 1), (0, 3),
    (2, 0), (1, 2), (2, 1), (1, 3), (3, 0), (2, 2),
    (3, 1), (2, 3), (4, 0), (3, 2), (4, 1), (3, 3),
    (5, 0), (4, 2), (5, 1), (4, 3), (6, 0), (5, 2),
    (6, 1), (5, 3), (7, 0), (6, 2), (7, 1), (6, 3),
    (8, 0), (7, 2), (8, 1), (7, 3), (8, 2), (8, 3),
)
MESH = pl.DeviceIdType.MESH
HIGHEST = lax.Precision.HIGHEST
F32 = jnp.float32
BF16 = jnp.bfloat16


def split3(value):
    hi = value.astype(BF16)
    rest = value - hi.astype(F32)
    mid = rest.astype(BF16)
    lo = (rest - mid.astype(F32)).astype(BF16)
    return hi, mid, lo


def dot(a, b, dims, precision=None):
    return lax.dot_general(
        a, b, (dims, ((), ())), precision=precision, preferred_element_type=F32
    )


def inverse_factor(gram):
    rank = gram.shape[0]
    rows = lax.broadcasted_iota(jnp.int32, (rank, rank), 0)
    cols = lax.broadcasted_iota(jnp.int32, (rank, rank), 1)
    eye = (rows == cols).astype(F32)
    work = jnp.concatenate([gram, eye], axis=1)
    below = lax.broadcasted_iota(jnp.int32, (rank, 1), 0)
    done = []
    for k in range(rank):
        first = (k // SUB) * SUB
        row = work[k - first : k - first + 1, :]
        factor = work[:, k : k + 1] / row[:, k : k + 1]
        factor = jnp.where(below[first:] > k, factor, 0.0)
        work = work - factor * row
        if k % SUB == SUB - 1:
            done.append(work[:SUB])
            work = work[SUB:]
    work = jnp.concatenate(done, axis=0)
    pivots = jnp.sum(work[:, :rank] * eye, axis=1, keepdims=True)
    return work[:, rank:] / jnp.sqrt(pivots)


def padded(per, zhalf):
    return -(-per // zhalf) * zhalf


def kernel(sizes, g_hbm, e_hbm, q_hbm, out_ref, qn_ref,
           g_ref, e_ref, turned, rq, acc, gacc, qt, weight, load, send, recv, *held):
    nx, ny, nz = sizes
    jcs = nx * ny // 2
    zhalf = nz // 2
    dp = lax.axis_index("dp")
    fs = lax.axis_index("fsdp")
    x = lax.rem(dp, nx)
    ylo = dp // nx
    yh = ny // YL
    core = lax.rem(fs, 2)
    yhi = lax.rem(fs // 2, yh)
    z = fs // (2 * yh)
    y = yhi * YL + ylo
    other = lax.rem(core + 1, 2)
    replicas = YL * nx
    count = len(BATCHES)
    starts = [sum(BATCHES[:b]) * jcs * LANES for b in range(count)]
    sizes_of = [per * jcs * LANES for per in BATCHES]
    p, o, r0, r1a, r1b, r2a, r2b, r3 = (
        held[n * count : (n + 1) * count] for n in range(8)
    )

    first_q = pltpu.make_async_copy(q_hbm, qt, load.at[2 * count])
    first_q.start()
    loads = []
    for b in range(count):
        rows = pl.ds(starts[b], sizes_of[b])
        for n, (src, dst) in enumerate(((g_hbm, g_ref), (e_hbm, e_ref))):
            copy = pltpu.make_async_copy(src.at[rows], dst.at[rows], load.at[2 * b + n])
            copy.start()
            loads.append(copy)

    def device(dx, dy, dz, dc):
        tx = lax.rem(x + dx, nx)
        ty = lax.rem(y + dy, ny)
        tz = lax.rem(z + dz, nz)
        tc = lax.rem(core + dc, 2)
        return (lax.rem(ty, YL) * nx + tx, (tz * yh + ty // YL) * 2 + tc)

    def replica(d):
        return (lax.rem(dp + d, replicas), fs)

    peers = [device(0, 0, 0, 1)]
    peers += [device(d, 0, 0, 0) for d in range(1, nx)]
    peers += [device(0, d, 0, 0) for d in range(1, ny)]
    peers += [device(0, 0, d, 0) for d in range(1, nz)]
    peers += [
        (lax.rem(ylo + 1, YL) * nx + lax.rem(x + d, nx), fs) for d in range(1, nx)
    ]
    barrier = pltpu.get_barrier_semaphore()
    for peer in peers:
        pl.semaphore_signal(barrier, inc=1, device_id=peer, device_id_type=MESH)

    for b, per in enumerate(BATCHES):
        pad = padded(per, zhalf) - per
        if pad:
            p[b][:, :, :, :, per:] = jnp.zeros((2, 2, 2, jcs, pad, SUB, LANES), F32)
    first_q.wait()
    pl.semaphore_wait(barrier, len(peers))

    def at(index):
        return index // jcs, lax.rem(index, jcs)

    mine = (at(x * ny + y), at(y * nx + x))

    def both(b, start, size):
        rows = pl.ds(pl.multiple_of(starts[b] + start, LANES), size)
        return jnp.concatenate([g_ref[rows, :], e_ref[rows, :]], axis=1)

    def z_block(ref, b, zz):
        part = zz // zhalf
        hi = part * mine[1][0] + (1 - part) * mine[0][0]
        jc = part * mine[1][1] + (1 - part) * mine[0][1]
        zt = padded(BATCHES[b], zhalf) // zhalf
        return ref[b].at[core, part, hi, jc, pl.ds(lax.rem(zz, zhalf) * zt, zt)]

    def row_of(ref, b, part, chip):
        hi, jc = at(chip * (ny, nx)[part])
        used = pl.ds(0, BATCHES[b])
        return ref[b].at[core, part, hi, pl.ds(jc, (ny, nx)[part]), used]

    def one_of(ref, b, part, index):
        hi, jc = at(index)
        return ref[b].at[core, part, hi, jc, pl.ds(0, BATCHES[b])]

    def far_first(n):
        return sorted(range(1, n), key=lambda d: -min(d, n - d))

    def one_iteration(it, carry):
        issued = [0]

        def push(src, dst, target):
            n = issued[0]
            issued[0] += 1
            copy = pltpu.make_async_remote_copy(
                src_ref=src, dst_ref=dst, send_sem=send.at[n], recv_sem=recv.at[n],
                device_id=target, device_id_type=MESH,
            )
            copy.start()
            return copy

        def finish(copies):
            for copy in copies:
                copy.wait()

        parts = split3(qt[...])
        left = jnp.concatenate(
            [jnp.concatenate([v, v], axis=1) for v in parts], axis=0
        )

        def project(b):
            per = BATCHES[b]
            wide = 2 * per * LANES

            def step(k, c):
                out = dot(left, both(b, k * wide, wide), ((1,), (1,)))
                out = out[:RANK] + out[RANK : 2 * RANK] + out[2 * RANK :]
                for j in range(2 * per):
                    tile = out[:, j * LANES : (j + 1) * LANES]
                    p[b][:, :, :, 2 * k + j // per, j % per] = tile.reshape(
                        2, 2, 2, SUB, LANES
                    )
                return c

            lax.fori_loop(0, jcs // 2, step, 0)

        def core_send(b):
            src = p[b].at[other, :, :, :, pl.ds(0, BATCHES[b])]
            return [push(src, r0[b], device(0, 0, 0, 1))]

        def core_add(b):
            def step(jc, c):
                p[b][core, :, :, jc, : BATCHES[b]] += r0[b][:, :, jc]
                return c

            lax.fori_loop(0, jcs, step, 0)

        firsts = ((x, nx, r1a), (y, ny, r1b))
        seconds = ((y, ny, r2a), (x, nx, r2b))

        def along(part, d):
            return device(d, 0, 0, 0) if part == 0 else device(0, d, 0, 0)

        def first_send(b, part):
            chip, n, got = firsts[part]
            copies = []
            for d in far_first(n):
                src = row_of(p, b, part, lax.rem(chip + d, n))
                copies.append(push(src, got[b].at[d - 1], along(part, d)))
            return copies

        def first_add(b, part):
            chip, n, got = firsts[part]
            target = row_of(p, b, part, chip)
            total = target[...]
            for d in range(n - 1):
                total = total + got[b][d]
            target[...] = total

        def second_send(b, part):
            chip, n, got = seconds[part]
            base = (x * ny, y * nx)[part]
            copies = []
            for d in far_first(n):
                src = one_of(p, b, part, base + lax.rem(chip + d, n))
                copies.append(push(src, got[b].at[d - 1], along(1 - part, d)))
            return copies

        def second_add(b, part):
            _, n, got = seconds[part]
            target = one_of(p, b, part, (x * ny + y, y * nx + x)[part])
            total = target[...]
            for d in range(n - 1):
                total = total + got[b][d]
            target[...] = total

        def z_send(b):
            copies = []
            for d in far_first(nz):
                src = z_block(p, b, lax.rem(z + d, nz))
                copies.append(push(src, r3[b].at[d - 1], device(0, 0, d, 0)))
            return copies

        def z_add(b):
            total = z_block(p, b, z)[...]
            for d in range(nz - 1):
                total = total + r3[b][d]
            z_block(o, b, z)[...] = total

        def z_spread(b):
            block = z_block(o, b, z)
            return [push(block, block, device(0, 0, d, 0)) for d in far_first(nz)]

        def second_spread(b, part):
            block = one_of(o, b, part, (x * ny + y, y * nx + x)[part])
            n = (ny, nx)[part]
            return [push(block, block, along(1 - part, d)) for d in far_first(n)]

        def first_spread(b, part):
            chip, n, _ = firsts[part]
            block = row_of(o, b, part, chip)
            return [push(block, block, along(part, d)) for d in far_first(n)]

        def core_spread(b, part):
            block = o[b].at[core, part, :, :, pl.ds(0, BATCHES[b])]
            return [push(block, block, device(0, 0, 0, 1))]

        def tiles_of(b, jc):
            return [
                o[b][:, :, :, jc, s].reshape(RANK, LANES) for s in range(BATCHES[b])
            ]

        def back(b):
            tiles = []
            for jc in range(jcs):
                tiles += tiles_of(b, jc)
            stack = jnp.concatenate(split3(jnp.concatenate(tiles, axis=1)), axis=0)
            acc[...] += dot(stack, both(b, 0, sizes_of[b]), ((1,), (0,)))
            gacc[...] += dot(stack, stack, ((1,), (1,)))

        def turn(b):
            @pl.when(it == ITERS - 1)
            def _():
                def step(jc, c):
                    for s, tile in enumerate(tiles_of(b, jc)):
                        hi = tile.astype(BF16).astype(F32)
                        pair = jnp.concatenate([hi, tile - hi], axis=0)
                        start = starts[b] + (jc * BATCHES[b] + s) * LANES
                        rows = pl.ds(pl.multiple_of(start, LANES), LANES)
                        turned[rows, :] = pair.T.astype(BF16)
                    return c

                lax.fori_loop(0, jcs, step, 0)

        def loaded(b):
            @pl.when(it == 0)
            def _():
                loads[2 * b].wait()
                loads[2 * b + 1].wait()

        acc[...] = jnp.zeros_like(acc)
        gacc[...] = jnp.zeros_like(gacc)
        flying = [None] * count

        def enter(b):
            loaded(b)
            project(b)

        def leave(b):
            back(b)
            if b < count - 1:
                turn(b)

        stages = (
            (enter, core_send, False),
            (core_add, first_send, True),
            (first_add, second_send, True),
            (second_add, z_send, False),
            (z_add, z_spread, False),
            (None, second_spread, True),
            (None, first_spread, True),
            (None, core_spread, True),
            (leave, None, False),
        )
        for step, b in ORDER:
            work, start, by_part = stages[step]
            before = step and stages[step - 1][2]
            if before and by_part:
                for part in range(2):
                    finish(flying[b][part])
                    if work is not None:
                        work(b, part)
                    flying[b][part] = start(b, part)
                continue
            if before:
                for part in range(2):
                    finish(flying[b][part])
                    if work is second_add:
                        work(b, part)
            elif step:
                finish(flying[b])
            if work is not None and work is not second_add:
                work(b)
            if by_part:
                flying[b] = [start(b, part) for part in range(2)]
            elif start is not None:
                flying[b] = start(b)

        right = acc[...]
        right = right[:, :LANES] + right[:, LANES:]
        right = right[:RANK] + right[RANK : 2 * RANK] + right[2 * RANK :]
        rq[dp] = right
        copies = [push(rq.at[dp], rq.at[dp], replica(d)) for d in range(1, replicas)]
        gram = gacc[...]
        gram = gram[:, :RANK] + gram[:, RANK : 2 * RANK] + gram[:, 2 * RANK :]
        gram = gram[:RANK] + gram[RANK : 2 * RANK] + gram[2 * RANK :]
        inverse = inverse_factor(gram / (replicas * replicas))
        turn(count - 1)
        finish(copies)
        right = rq[0]
        for d in range(1, replicas):
            right = right + rq[d]
        right = right / (replicas * replicas)
        q_next = dot(inverse, right, ((1,), (0,)), HIGHEST)
        qt[...] = q_next

        @pl.when(it == ITERS - 1)
        def _():
            qn_ref[...] = q_next
            weight[...] = dot(inverse, q_next, ((0,), (0,)), HIGHEST) / replicas

        return carry

    lax.fori_loop(0, ITERS, one_iteration, 0)
    hi, mid, _ = split3(weight[...])
    right = jnp.concatenate([hi, hi, mid, jnp.zeros_like(hi)], axis=0)
    span = 2 * sum(BATCHES) * LANES

    def subtract(k, c):
        rows = pl.ds(pl.multiple_of(k * span, span), span)
        left = turned[rows, :]
        update = dot(jnp.concatenate([left, left], axis=1), right, ((1,), (0,)))
        accum = g_ref[rows, :].astype(F32) + e_ref[rows, :].astype(F32)
        out_ref[rows, :] = (accum - update).astype(BF16)
        return c

    lax.fori_loop(0, jcs // 2, subtract, 0)


def on_device(sizes, gradient, error_buffer, q_start):
    nx, ny, nz = sizes
    jcs = nx * ny // 2
    zhalf = nz // 2
    replicas = YL * nx
    count = len(BATCHES)
    per_batch = 3 + 4 * (nx - 1) + 4 * (ny - 1) + 2 * (nz - 1)
    copies = count * per_batch + replicas - 1
    vmem = pl.BlockSpec(memory_space=pltpu.VMEM)
    hbm = pl.BlockSpec(memory_space=pltpu.HBM)
    tile = (SUB, LANES)
    gradient, error_buffer = gradient[0], error_buffer[0]
    rows = gradient.shape[0]
    whole = pltpu.VMEM((rows, LANES), BF16)
    slots = [padded(per, zhalf) for per in BATCHES]
    held = [pltpu.VMEM((2, 2, 2, jcs, s) + tile, F32) for s in slots] * 2
    held += [pltpu.VMEM((2, 2, jcs, s) + tile, F32) for s in BATCHES]
    held += [pltpu.VMEM((nx - 1, ny, s) + tile, F32) for s in BATCHES]
    held += [pltpu.VMEM((ny - 1, nx, s) + tile, F32) for s in BATCHES]
    held += [pltpu.VMEM((ny - 1, s) + tile, F32) for s in BATCHES]
    held += [pltpu.VMEM((nx - 1, s) + tile, F32) for s in BATCHES]
    held += [pltpu.VMEM((nz - 1, s // zhalf) + tile, F32) for s in slots]
    small = jax.ShapeDtypeStruct((RANK, LANES), F32)
    new_error, q_factor = pl.pallas_call(
        functools.partial(kernel, sizes),
        out_shape=(jax.ShapeDtypeStruct(gradient.shape, BF16), small),
        in_specs=[hbm] * 3,
        out_specs=(vmem, vmem),
        scratch_shapes=[
            whole,
            whole,
            whole,
            pltpu.VMEM((replicas, RANK, LANES), F32),
            pltpu.VMEM((3 * RANK, 2 * LANES), F32),
            pltpu.VMEM((3 * RANK, 3 * RANK), F32),
            pltpu.VMEM((RANK, LANES), F32),
            pltpu.VMEM((RANK, LANES), F32),
            pltpu.SemaphoreType.DMA((2 * count + 1,)),
            pltpu.SemaphoreType.DMA((copies,)),
            pltpu.SemaphoreType.DMA((copies,)),
        ] + held,
        compiler_params=pltpu.CompilerParams(
            collective_id=0, has_side_effects=True, vmem_limit_bytes=40 * 2**20
        ),
        cost_estimate=pl.CostEstimate(
            flops=8 * rows * LANES * RANK, bytes_accessed=6 * rows * LANES,
            transcendentals=0,
        ),
    )(*[
        pltpu.with_memory_space_constraint(value, pltpu.HBM)
        for value in (gradient, error_buffer, q_start.T)
    ])
    return (new_error[None], q_factor.T)


def solution(mesh, sizes=(4, 4, 8)):
    in_specs = (P("dp", None, "fsdp"), P("dp", None, "fsdp"), P("fsdp", None))
    out_specs = (P("dp", None, "fsdp"), P("fsdp", None))
    return jax.shard_map(
        functools.partial(on_device, sizes), mesh=mesh, in_specs=in_specs,
        out_specs=out_specs, check_vma=False,
    )
```
